512 devices in a mesh: rep: 4 (over z_lo), tab: 8 (over z_hi, core), fsdp: 16 (over y, x).
Axes of the slice: x: 4, y: 4, z: 16 (z_hi: 4, z_lo: 4; z = z_hi * 4 + z_lo), core: 2. Of those that a mesh axis runs over, the one named last changes fastest.
Arguments:
- pooled: bfloat16 [16384, 128, 192], P(('rep', 'tab', 'fsdp')), may hold values from -6 to 6
- projection: bfloat16 [128, 16], replicated, may hold values from -0.0390625 to 0.0390625
- w_inner: bfloat16 [2048, 1024], P('fsdp'), may hold values from -0.125 to 0.125
- w_outer: bfloat16 [1024, 1536], P(None, 'fsdp'), may hold values from -0.1875 to 0.1875
- upstream: bfloat16 [16384, 1536], P(('rep', 'tab', 'fsdp')), may hold values from -24 to 24
- feature_order: int32 [128], replicated, may hold values from 0 to 127, each once
- bag_slots: int32 [4, 8, 512, 128, 4], P('rep', None, 'fsdp', 'tab'), may hold values from 0 to 1023
- bag_lengths: int32 [4, 8, 512, 128], P('rep', None, 'fsdp', 'tab'), may hold values from 1 to 4
Outputs:
- grad_inner: float32 [2048, 1024], P('fsdp')
- grad_outer: float32 [1024, 1536], P(None, 'fsdp')
- grad_proj: float32 [128, 16], replicated
- row_grads: float32 [8, 16, 1024, 192], P('tab', 'fsdp', 'rep')
The draws below stay inside these ranges and needn't reach their ends.
Inputs may be any that keep to these rules, and one draw needn't show every extreme that they name: `bag_slots`: index into the deduplicated row list of the owning table shard; all replica groups share that list. `bag_lengths`: slots of a bag past its length are ignored. `feature_order`: each feature once.
All inputs are finite; a program needn't handle non-finite values.
Results may differ from the reference program's by a relative error of at most 0.03.
Values may be sent and summed in bfloat16 or wider, within the bound.
No kernel may reach another device: no remote copies, remote signals or barrier semaphores. Data moves between devices by JAX's collectives and lax.ppermute only.
A program may use at most 64 MiB of HBM per device.

```python
import math
import jax
import jax.numpy as jnp
from jax import lax

NFEAT = 128
EMB = 192
RANK = 16
MLP_UNITS = 1024
BAG = 4
B_DEV = 32
DEDUP = 1024
FLAT = 2048
OUTW = 1536
FOWN = 16
BATCH = 16384
N_REP = 4
N_TAB = 8
N_FSDP = 16


def plant(entries, rng, least, top_value):
    extent = entries.shape
    spot = [jax.random.randint(jax.random.fold_in(rng, axis), (), 0, extent[axis]) for axis in range(len(extent))]
    entries = entries.at[tuple(spot)].set(least)
    longest = extent.index(max(extent))
    spot[longest] = (spot[longest] + 1) % extent[longest]
    return entries.at[tuple(spot)].set(top_value)


def strengthened(entries, stream_key, source, target, blocks, factor):
    def block_of(dim):
        return (jnp.arange(entries.shape[dim]) // (entries.shape[dim] // blocks)).reshape((-1,) + (1,) * (entries.ndim - 1 - dim))

    near = jax.random.permutation(stream_key, blocks)[block_of(target)]
    second = (block_of(target) + blocks // 2) % blocks
    return jnp.where((block_of(source) == near) | (block_of(source) == second), factor * entries, entries)


def level_of(key, extent, split, least, top_value):
    def one(axis_at, parts):
        draws = jax.random.uniform(jax.random.fold_in(jax.random.fold_in(key, 6), axis_at), (parts,), jnp.float32, least / len(split), top_value / len(split))
        return jnp.repeat(jnp.exp(draws), extent[axis_at] // parts).reshape((-1,) + (1,) * (len(extent) - axis_at - 1))

    level = one(*split[0])
    for cut in split[1:]:
        level = level * one(*cut)
    return level


def centred(stream_key, extent, spread, bound, cuts=(), kind=jnp.bfloat16):
    result = jax.random.normal(stream_key, extent, jnp.float32) * spread
    if len(cuts) > 0:
        result = level_of(stream_key, extent, cuts, -0.22, 0.18) * result
    return jnp.clip(result, min=-bound, max=bound).astype(kind)


def bell_draw_with(key, extent, spread, limit, split, heavy, kind=jnp.bfloat16):
    result = spread * jax.random.normal(key, extent, jnp.float32)
    if split:
        result = result * level_of(key, extent, split, -0.22, 0.18)
    return jnp.clip(strengthened(result, jax.random.fold_in(key, 3), *heavy), -limit, limit).astype(kind)


def setup_inputs(seed: int = 0) -> dict:
    seeds = jax.random.split(jax.random.key(seed), 9)
    pooled = centred(seeds[0], (BATCH, NFEAT, EMB), 1.0, 6.0, ((0, 512),))
    projection = centred(seeds[1], (NFEAT, RANK), (NFEAT * EMB) ** -0.5, 0.0390625)
    w_inner = centred(seeds[2], (FLAT, MLP_UNITS), FLAT ** -0.5, 0.125, ((0, 16),))
    w_outer = centred(seeds[3], (MLP_UNITS, OUTW), MLP_UNITS ** -0.5, 0.1875, ((1, 16),))
    upstream = bell_draw_with(seeds[4], (BATCH, OUTW), 1.0, 24.0, ((0, 512),), (0, 1, 512, 6.0))
    feature_order = jax.random.permutation(seeds[5], NFEAT).astype(jnp.int32)
    bag_slots = plant(jax.random.randint(seeds[6], (N_REP, N_TAB, N_FSDP * B_DEV, NFEAT, BAG), 0, DEDUP), jax.random.fold_in(seeds[6], 1), 0, DEDUP - 1).astype(jnp.int32)
    bag_lengths = plant(jax.random.randint(seeds[7], (N_REP, N_TAB, N_FSDP * B_DEV, NFEAT), 1, BAG + 1), jax.random.fold_in(seeds[7], 1), 1, BAG).astype(jnp.int32)
    return dict(pooled=pooled, projection=projection, w_inner=w_inner, w_outer=w_outer, upstream=upstream, feature_order=feature_order, bag_slots=bag_slots, bag_lengths=bag_lengths)


def block_grads(sample_block, upstream_block, projection, w_inner, w_outer):
    pooled_f = sample_block.astype(jnp.float32)
    proj_f = projection.astype(jnp.float32)
    compress = jnp.einsum('bfe,fk->bek', pooled_f, proj_f).astype(jnp.bfloat16)
    zed = jnp.einsum('bfe,bek->bfk', pooled_f, compress.astype(jnp.float32)).astype(jnp.bfloat16)
    samples = sample_block.shape[0]
    flattened = zed.reshape(samples, FLAT)
    preact = jnp.dot(flattened, w_inner, preferred_element_type=jnp.float32)
    logistic = jax.nn.sigmoid(preact)
    activated = (preact * logistic).astype(jnp.bfloat16)
    grad_act = jnp.dot(upstream_block, w_outer.T, preferred_element_type=jnp.float32)
    grad_pre = (grad_act * (logistic * (1.0 + preact * (1.0 - logistic)))).astype(jnp.bfloat16)
    grad_flat = jnp.dot(grad_pre, w_inner.T, preferred_element_type=jnp.float32).astype(jnp.bfloat16)
    grad_zed = grad_flat.reshape(samples, NFEAT, RANK).astype(jnp.float32)
    grad_comp = jnp.einsum('bfe,bfk->bek', pooled_f, grad_zed).astype(jnp.bfloat16)
    grad_comp_f = grad_comp.astype(jnp.float32)
    pooled_grad = (jnp.einsum('bfk,bek->bfe', grad_zed, compress.astype(jnp.float32)) + jnp.einsum('fk,bek->bfe', proj_f, grad_comp_f)).astype(jnp.bfloat16)
    part_inner = jnp.dot(flattened.T, grad_pre, preferred_element_type=jnp.float32)
    part_outer = jnp.dot(activated.T, upstream_block, preferred_element_type=jnp.float32)
    part_proj = jnp.einsum('bfe,bek->fk', pooled_f, grad_comp_f)
    return (pooled_grad, part_inner, part_outer, part_proj)

def rounded(values):
    return lax.optimization_barrier(values.astype(jnp.bfloat16)).astype(jnp.float32)

def reference(pooled, projection, w_inner, w_outer, upstream, feature_order, bag_slots, bag_lengths):
    group_size = N_FSDP * B_DEV
    blocks = pooled.reshape(N_REP * N_TAB, group_size, NFEAT, EMB)
    upper = upstream.reshape(N_REP * N_TAB, group_size, OUTW)

    def step(carry, inputs):
        sum_inner, sum_outer, sum_proj = carry
        pooled_grad, part_inner, part_outer, part_proj = block_grads(inputs[0], inputs[1], projection, w_inner, w_outer)
        carry = (sum_inner + rounded(part_inner), sum_outer + rounded(part_outer), sum_proj + part_proj)
        return (carry, pooled_grad)
    start = (jnp.zeros((FLAT, MLP_UNITS), jnp.float32), jnp.zeros((MLP_UNITS, OUTW), jnp.float32), jnp.zeros((NFEAT, RANK), jnp.float32))
    (sum_inner, sum_outer, sum_proj), grads = lax.scan(step, start, (blocks, upper))
    loss_scale = 1.0 / math.sqrt(BATCH)
    grad_inner = sum_inner * loss_scale
    grad_outer = sum_outer * loss_scale
    grad_proj = sum_proj * loss_scale
    grads = grads.reshape(N_REP, N_TAB * N_FSDP * B_DEV, NFEAT, EMB)
    total_rows = N_TAB * N_FSDP * DEDUP
    owner_ids = jnp.arange(N_TAB, dtype=jnp.int32).reshape(1, 1, 1, N_TAB, 1)
    shard_ids = jnp.arange(N_FSDP, dtype=jnp.int32).reshape(1, N_FSDP, 1, 1, 1)
    row_base = (owner_ids * N_FSDP + shard_ids) * DEDUP
    row_grads = jnp.zeros((total_rows, EMB), jnp.float32)
    for replica in range(N_REP):
        ordered = grads[replica][:, feature_order, :]
        ordered = ordered.reshape(N_TAB, N_FSDP, B_DEV, N_TAB, FOWN, EMB)
        values = ordered.astype(jnp.float32).reshape(-1, EMB)
        slots_r = bag_slots[replica].reshape(N_TAB, N_FSDP, B_DEV, N_TAB, FOWN, BAG)
        lengths_r = bag_lengths[replica].reshape(N_TAB, N_FSDP, B_DEV, N_TAB, FOWN)
        running = jnp.zeros((total_rows, EMB), jnp.float32)
        for slot_index in range(BAG):
            row_ids = jnp.where(slot_index < lengths_r, slots_r[..., slot_index] + row_base, total_rows)
            running = running + jax.ops.segment_sum(values, row_ids.reshape(-1).astype(jnp.int32), num_segments=total_rows)
        row_grads = row_grads + rounded(running)
    row_grads = row_grads.reshape(N_TAB, N_FSDP, DEDUP, EMB)
    return (grad_inner, grad_outer, grad_proj, row_grads)
```

```python
import math

import jax
import jax.numpy as jnp
from jax import lax
from jax.experimental import pallas as pl
from jax.experimental.pallas import tpu as pltpu
from jax.sharding import PartitionSpec as P

DEDUP = 1024
BF = jnp.bfloat16
F32 = jnp.float32
ZT = ("rep", "tab")
N_REP, N_TAB = 4, 8
TEAM = [[(2 * a + b) * 8 + 2 * h + c for b in range(2) for c in range(2)] for a in range(2) for h in range(4)]
PEERS = [[(2 * a + b) * 8 + 2 * h + c for a in range(2) for h in range(4)] for b in range(2) for c in range(2)]


def exchange(pieces, axis, groups=None):
    return lax.all_to_all(pieces, axis, 0, 0, axis_index_groups=groups)


def spread(block, count, axis, groups=None):
    return exchange(jnp.broadcast_to(block[None], (count,) + block.shape), axis, groups)


def swap(block, k):
    pairs = [(r * 8 + t, (r ^ (k >> 1)) * 8 + (t ^ (k & 1))) for r in range(N_REP) for t in range(N_TAB)]
    return lax.ppermute(block, ZT, pairs)


def pooled_kernel(left_ref, right_ref, *out_refs):
    samples = left_ref.shape[0]
    half = samples // 2

    def step(i, _):
        both = []
        for sample in (i, i + half):
            grads = jnp.dot(left_ref[sample], right_ref[sample], preferred_element_type=F32).astype(BF)
            rows = pl.ds(pl.multiple_of(sample * 16, 16), 16)
            for k, out_ref in enumerate(out_refs):
                out_ref[rows, :] = grads[16 * k : 16 * k + 16, :128]
            both.append(grads[:, 128:])
        tail = jnp.concatenate(both, axis=1)
        rows = pl.ds(pl.multiple_of(samples * 16 + i * 16, 16), 16)
        for k, out_ref in enumerate(out_refs):
            out_ref[rows, :] = tail[16 * k : 16 * k + 16, :]
        return 0

    lax.fori_loop(0, half, step, 0)


def pooled_grads(left, right):
    samples = left.shape[0]
    return pl.pallas_call(
        pooled_kernel,
        out_shape=[jax.ShapeDtypeStruct((samples * 24, 128), BF)] * 8,
        in_specs=[pl.BlockSpec(memory_space=pltpu.VMEM)] * 2,
        out_specs=[pl.BlockSpec(memory_space=pltpu.VMEM)] * 8,
        compiler_params=pltpu.CompilerParams(vmem_limit_bytes=16 * 1024 * 1024),
        cost_estimate=pl.CostEstimate(flops=2 * samples * 128 * 256 * 128, bytes_accessed=4 << 20, transcendentals=0),
        name="pooled_grads",
    )(left, right)


def counts_kernel(index_ref, slots_ref, out_ref):
    rows = out_ref.shape[1]
    base = pl.program_id(1) * rows
    ids = lax.broadcasted_iota(jnp.int32, (rows, out_ref.shape[2]), 0) + base
    total = jnp.zeros(ids.shape, F32)
    for bag in range(4):
        total = total + jnp.where(ids == slots_ref[0, bag : bag + 1, :], 1.0, 0.0)
    out_ref[0] = total.astype(BF)


def slot_counts(index, slots):
    sources, _, width = slots.shape
    return pl.pallas_call(
        counts_kernel,
        grid_spec=pltpu.PrefetchScalarGridSpec(
            num_scalar_prefetch=1,
            grid=(sources, 4),
            in_specs=[pl.BlockSpec((1, 4, width), lambda s, m, index: (index[s], 0, 0))],
            out_specs=pl.BlockSpec((1, DEDUP // 4, width), lambda s, m, index: (s, m, 0)),
        ),
        out_shape=jax.ShapeDtypeStruct((sources, DEDUP, width), BF),
        compiler_params=pltpu.CompilerParams(vmem_limit_bytes=16 * 1024 * 1024),
        cost_estimate=pl.CostEstimate(flops=20 << 20, bytes_accessed=16 << 20, transcendentals=0),
        name="slot_counts",
    )(index, slots)


def segment_kernel(counts_ref, *refs):
    value_refs, (out_ref, total_ref) = refs[:8], refs[8:]
    source = pl.program_id(0)
    half = counts_ref.shape[2] // 2

    @pl.when(source == 0)
    def _():
        total_ref[...] = jnp.zeros_like(total_ref)

    for k, values_ref in enumerate(value_refs):

        @pl.when(source == k)
        def _(values_ref=values_ref):
            tail = values_ref[2 * half :, :]
            for part in range(2):
                head = values_ref[part * half : (part + 1) * half, :]
                total_ref[part] += jnp.dot(
                    counts_ref[0, :, part * half : (part + 1) * half],
                    jnp.concatenate([head, tail], axis=1),
                    preferred_element_type=F32,
                )

    @pl.when(source == pl.num_programs(0) - 1)
    def _():
        out_ref[:, :128] = (total_ref[0, :, :128] + total_ref[1, :, :128]).astype(BF)
        out_ref[:, 128:] = (total_ref[0, :, 128:192] + total_ref[1, :, 192:]).astype(BF)


def segment_sums(counts, values):
    sources, _, width = counts.shape
    return pl.pallas_call(
        segment_kernel,
        grid=(sources,),
        out_shape=jax.ShapeDtypeStruct((DEDUP, 192), BF),
        in_specs=[pl.BlockSpec((1, DEDUP, width), lambda s: (s, 0, 0))]
        + [pl.BlockSpec(memory_space=pltpu.VMEM)] * 8,
        out_specs=pl.BlockSpec((DEDUP, 192), lambda s: (0, 0)),
        scratch_shapes=[pltpu.VMEM((2, DEDUP, 256), F32)],
        compiler_params=pltpu.CompilerParams(vmem_limit_bytes=16 * 1024 * 1024),
        cost_estimate=pl.CostEstimate(flops=2 << 30, bytes_accessed=10 << 20, transcendentals=0),
        name="segment_sums",
    )(counts, *values)


def body(pooled, projection, w_inner, w_outer, upstream, feature_order, bag_slots, bag_lengths):
    samples, features, emb_width = pooled.shape
    rank = projection.shape[1]
    shards = lax.axis_size("fsdp")
    in_rows, units = w_inner.shape
    out_cols = w_outer.shape[1]
    flat, width = in_rows * shards, out_cols * shards
    grad_rows = in_rows + out_cols
    quarter = units // 4
    rep, tab = lax.axis_index("rep"), lax.axis_index("tab")
    far, core = tab // 2, tab % 2
    place = 2 * rep + core
    mine = place % 4

    weights = jnp.concatenate(
        [
            lax.dynamic_slice(w_inner, (0, mine * quarter), (in_rows, quarter)),
            lax.dynamic_slice(w_outer.T, (0, mine * quarter), (out_cols, quarter)),
        ]
    )
    weights = spread(weights, shards, "fsdp")
    inner = weights[:, :in_rows].reshape(flat, quarter)
    outer = weights[:, in_rows:].reshape(width, quarter)

    compress = jnp.einsum("bfe,fk->bek", pooled, projection, preferred_element_type=F32).astype(BF)
    zed = jnp.einsum("bfe,bek->bfk", pooled, compress, preferred_element_type=F32).astype(BF)
    joined = jnp.concatenate([zed.reshape(samples, flat), upstream], axis=1)

    bag = bag_slots.shape[-1]
    live = jnp.where(jnp.arange(bag) < bag_lengths[..., None], bag_slots, -1)
    live = live.reshape(4, 2, samples * 16, bag).transpose(0, 1, 3, 2)
    live, _ = lax.optimization_barrier((live, joined))
    near = []
    for k in range(4):
        piece = lax.dynamic_index_in_dim(live, rep ^ k, 0, False)
        near.append(lax.ppermute(piece, "rep", [(r, r ^ k) for r in range(4)]) if k else piece)
    across = [(r * 8 + 2 * f + c, f * 8 + 2 * r + c) for r in range(4) for f in range(4) for c in range(2)]
    slots = lax.ppermute(jnp.concatenate(near), ZT, across)
    sources = place ^ jnp.arange(8, dtype=jnp.int32)
    slot_index = (far ^ (sources // 2)) * 2 + sources % 2

    joined = jnp.concatenate([joined] + [swap(joined, k) for k in (1, 2, 3)], axis=0)
    joined, slots = lax.optimization_barrier((joined, slots))
    zed_all, up_all = joined[:, :flat], joined[:, flat:]

    preact = jnp.dot(zed_all, inner, preferred_element_type=F32)
    logistic = jax.nn.sigmoid(preact)
    activated = (preact * logistic).astype(BF)
    grad_act = jnp.dot(up_all, outer, preferred_element_type=F32)
    grad_pre = (grad_act * (logistic * (1.0 + preact * (1.0 - logistic)))).astype(BF)

    partial_zed = lax.dot_general(grad_pre, inner, (((1,), (1,)), ((), ())), preferred_element_type=F32).astype(BF)
    partial_zed = partial_zed.reshape(4, samples, flat)
    grad_zed = partial_zed[0].astype(F32)
    for k in (1, 2, 3):
        grad_zed = grad_zed + swap(partial_zed[k], k).astype(F32)
    grad_zed = grad_zed.astype(BF).reshape(samples, features, rank)

    grad_comp = jnp.einsum("bfe,bfk->bek", pooled, grad_zed, preferred_element_type=F32).astype(BF)
    order = feature_order.reshape(8, 16)
    order = jnp.concatenate([lax.dynamic_index_in_dim(order, place ^ k, 0, False) for k in range(8)])
    order = (order[:, None] == jnp.arange(features)[None, :]).astype(BF)
    ordered_zed = jnp.einsum("jf,bfk->bjk", order, grad_zed, preferred_element_type=F32).astype(BF)
    ordered_proj = jnp.dot(order, projection, preferred_element_type=F32).astype(BF)
    left = jnp.concatenate(
        [ordered_zed, jnp.broadcast_to(ordered_proj[None], (samples, features, rank))], axis=2
    )
    right = jnp.concatenate([compress, grad_comp], axis=2).transpose(0, 2, 1)
    routed = pooled_grads(left, right)
    slots, _ = lax.optimization_barrier((slots, routed[0]))
    counts = slot_counts(slot_index, slots)
    own_rows = routed[0]
    routed = [routed[0]] + [swap(routed[k], k) for k in range(1, 8)]
    sums = segment_sums(counts, routed).reshape(4, DEDUP // 4, emb_width)
    row_share = jnp.zeros((DEDUP // 4, emb_width), F32)
    for k in range(4):
        pairs = [
            (r * 8 + 2 * f + c, ((f + k) % 4) * 8 + 2 * r + c) for r in range(4) for f in range(4) for c in range(2)
        ]
        piece = lax.dynamic_index_in_dim(sums, (far + k) % 4, 0, False)
        row_share = row_share + lax.ppermute(piece, ZT, pairs).astype(F32)

    over_samples = (((0,), (0,)), ((), ()))
    part_inner = lax.dot_general(zed_all, grad_pre, over_samples, preferred_element_type=F32).astype(BF)
    part_outer = lax.dot_general(up_all, activated, over_samples, preferred_element_type=F32).astype(BF)
    parts = jnp.concatenate(
        [part_inner.reshape(shards, in_rows, quarter), part_outer.reshape(shards, out_cols, quarter)], axis=1
    )
    parts, _ = lax.optimization_barrier((exchange(parts, "fsdp"), own_rows))
    parts = jnp.sum(parts.astype(F32), axis=0).astype(BF)
    part_proj = jnp.einsum("bfe,bek->kf", pooled, grad_comp, preferred_element_type=F32)
    part_proj, _ = lax.optimization_barrier((part_proj, parts))
    proj_rows = jnp.sum(spread(part_proj, shards, "fsdp"), axis=0).reshape(8, 1, -1)
    proj_high = proj_rows.astype(BF)
    proj_low = (proj_rows - proj_high.astype(F32)).astype(BF)
    pieces = jnp.concatenate([parts.reshape(8, grad_rows // 8, quarter), proj_high, proj_low], axis=1)
    share = jnp.sum(exchange(pieces, ZT, PEERS).astype(F32), axis=0)
    proj_share = share[-2:-1] + share[-1:]
    share_high = proj_share.astype(BF)
    share_low = (proj_share - share_high.astype(F32)).astype(BF)
    share = spread(jnp.concatenate([share[:-2].astype(BF), share_high, share_low]), 8, ZT, PEERS)
    quarters = lax.all_gather(share, ZT, axis_index_groups=TEAM)
    proj_sum = jnp.sum(quarters[:, :, -2, :].astype(F32) + quarters[:, :, -1, :].astype(F32), axis=0)
    proj_sum = proj_sum.reshape(rank, features).T
    grads = quarters[:, :, :-2, :].reshape(4, grad_rows, quarter).transpose(1, 0, 2).reshape(grad_rows, units)

    all_samples = samples * lax.axis_size("rep") * lax.axis_size("tab") * lax.axis_size("fsdp")
    loss_scale = 1.0 / math.sqrt(all_samples)
    grad_inner = grads[:in_rows].astype(F32) * loss_scale
    grad_outer = (grads[in_rows:].astype(F32) * loss_scale).T
    grad_proj = proj_sum * loss_scale
    row_grads = row_share.reshape(1, 1, DEDUP // 4, emb_width)
    return (grad_inner, grad_outer, grad_proj, row_grads)


def solution(mesh):
    in_specs = (
        P(("rep", "tab", "fsdp"), None, None),
        P(),
        P("fsdp", None),
        P(None, "fsdp"),
        P(("rep", "tab", "fsdp"), None),
        P(),
        P("rep", None, "fsdp", "tab", None),
        P("rep", None, "fsdp", "tab"),
    )
    out_specs = (P("fsdp", None), P(None, "fsdp"), P(), P("tab", "fsdp", "rep", None))
    return jax.shard_map(body, mesh=mesh, in_specs=in_specs, out_specs=out_specs, check_vma=False)
```

```python
import functools
import math

import jax
import jax.numpy as jnp
from jax import lax
from jax.experimental import pallas as pl
from jax.experimental.pallas import tpu as pltpu
from jax.sharding import PartitionSpec as P

DEDUP = 1024
BF = jnp.bfloat16
F32 = jnp.float32
ZT = ("rep", "tab")
N_REP, N_TAB = 4, 8
TEAM = [[(2 * a + b) * 8 + 2 * h + c for b in range(2) for c in range(2)] for a in range(2) for h in range(4)]
QUAD = [[r * 8 + 2 * h + c for r in range(4) for c in range(2)] for h in range(4)]
FAR = [[r * 8 + 2 * h + c for h in range(4)] for r in range(4) for c in range(2)]


def target(quad, rep, core):
    middle = 0 if (rep == 1) == (core == 0) else 2
    return (quad + {0: 3, 3: 1}.get(rep, middle)) % 4


OWNERS = [[2 * target(h, r, c) + c for r in range(4) for c in range(2)] for h in range(4)]
DEVICES = [(h, r, c) for h in range(4) for r in range(4) for c in range(2)]


def flat_id(quad, rep, core):
    return rep * 8 + 2 * quad + core


def exchange(pieces, axis, groups=None):
    return lax.all_to_all(pieces, axis, 0, 0, axis_index_groups=groups)


def spread(block, count, axis, groups=None):
    return exchange(jnp.broadcast_to(block[None], (count,) + block.shape), axis, groups)


def high_low(values, axis):
    high = values.astype(BF)
    return jnp.concatenate([high, (values - high.astype(F32)).astype(BF)], axis=axis)


def swap(block, k):
    pairs = [(r * 8 + t, (r ^ (k >> 1)) * 8 + (t ^ (k & 1))) for r in range(N_REP) for t in range(N_TAB)]
    return lax.ppermute(block, ZT, pairs)


def pooled_kernel(grads_ref, compress_ref, comp_ref, order_ref, proj_ref, out_ref, ordered_ref):
    samples = compress_ref.shape[0]
    half = samples // 2
    rank = proj_ref.shape[0]
    down = (((0,), (0,)), ((), ()))
    whole = grads_ref[...].reshape(samples * rank, 128)
    ordered = jnp.dot(whole, order_ref[...], preferred_element_type=F32).astype(BF)
    ordered_ref[...] = ordered.reshape(samples, rank, 128)

    def step(i, _):
        both = []
        for sample in (i, i + half):
            left = jnp.concatenate([ordered_ref[sample], proj_ref[...]], axis=0)
            right = jnp.concatenate([compress_ref[sample], comp_ref[sample]], axis=0)
            grads = lax.dot_general(left, right, down, preferred_element_type=F32).astype(BF)
            rows = pl.ds(pl.multiple_of(sample * 16, 16), 16)
            for p in range(8):
                out_ref[p, rows, :] = grads[16 * p : 16 * p + 16, :128]
            both.append(grads[:, 128:])
        tail = jnp.concatenate(both, axis=1)
        rows = pl.ds(pl.multiple_of(samples * 16 + i * 16, 16), 16)
        for p in range(8):
            out_ref[p, rows, :] = tail[16 * p : 16 * p + 16, :]
        return _

    lax.fori_loop(0, half, step, jnp.int32(0), unroll=4)
    first = samples * 24
    out_ref[:, first:, :] = jnp.zeros((8, out_ref.shape[1] - first, 128), BF)


def pooled_grads(grad_zed, compress, grad_comp, order, proj, grad_rows):
    samples, rank, _ = grad_zed.shape
    chunk = chunk_rows(grad_rows, samples * 24)
    whole = pl.BlockSpec(memory_space=pltpu.VMEM)
    return pl.pallas_call(
        pooled_kernel,
        out_shape=jax.ShapeDtypeStruct((8, samples * 24 + 2 * chunk, 128), BF),
        in_specs=[whole] * 5,
        out_specs=whole,
        scratch_shapes=[pltpu.VMEM((samples, rank, 128), BF)],
        compiler_params=pltpu.CompilerParams(vmem_limit_bytes=12 * 1024 * 1024),
        cost_estimate=pl.CostEstimate(flops=2 * samples * 128 * 256 * 128, bytes_accessed=6 << 20, transcendentals=0),
        name="pooled_grads",
    )(grad_zed, compress, grad_comp, order, proj)


def chunk_rows(grad_rows, first):
    return next(c for c in range(16, first, 16) if 8 * c >= grad_rows and first % (2 * c) == 0)


def chunk_kernel(parts_ref, routed_ref, out_ref):
    del routed_ref
    grad_rows = parts_ref.shape[1]
    chunk = out_ref.shape[1] // 2
    for p in range(8):
        rows = min(chunk, grad_rows - p * chunk)
        if rows <= 0:
            out_ref[p] = jnp.zeros((2 * chunk, 128), BF)
            continue
        total = jnp.sum(parts_ref[:, p * chunk : p * chunk + rows, :].astype(F32), axis=0).astype(BF)
        out_ref[p, :rows, :] = total[:, :128]
        out_ref[p, chunk : chunk + rows, :] = total[:, 128:]


def with_chunks(routed, parts, first):
    chunk = chunk_rows(parts.shape[1], first)
    return pl.pallas_call(
        chunk_kernel,
        grid=(1,),
        out_shape=jax.ShapeDtypeStruct(routed.shape, BF),
        in_specs=[pl.BlockSpec(parts.shape, lambda i: (0, 0, 0)), pl.BlockSpec(memory_space=pl.ANY)],
        out_specs=pl.BlockSpec((8, 2 * chunk, 128), lambda i: (0, first // (2 * chunk), 0)),
        input_output_aliases={1: 0},
        compiler_params=pltpu.CompilerParams(vmem_limit_bytes=10 * 1024 * 1024),
        cost_estimate=pl.CostEstimate(flops=1 << 20, bytes_accessed=2 << 20, transcendentals=0),
        name="with_chunks",
    )(parts, routed)


def middle_kernel(shards, in_rows, weights_ref, *refs):
    pieces, (parts_ref, *partial_refs), joined = refs[:4], refs[4:9], refs[9]
    samples = pieces[0].shape[0]
    flat = shards * in_rows
    out_cols = weights_ref.shape[1] - in_rows
    step = 4 if shards % 4 == 0 else 1
    for k, piece in enumerate(pieces):
        joined[k * samples : (k + 1) * samples, :] = piece[...]

    def inner(g):
        return weights_ref[g : g + step, :in_rows, :].reshape(step * in_rows, -1)

    preact = jnp.zeros((4 * samples, weights_ref.shape[2]), F32)
    grad_act = jnp.zeros_like(preact)
    for g in range(0, shards, step):
        preact += jnp.dot(joined[:, g * in_rows : (g + step) * in_rows], inner(g), preferred_element_type=F32)
        grad_act += jnp.dot(
            joined[:, flat + g * out_cols : flat + (g + step) * out_cols],
            weights_ref[g : g + step, in_rows:, :].reshape(step * out_cols, -1),
            preferred_element_type=F32,
        )
    logistic = jax.nn.sigmoid(preact)
    activated = (preact * logistic).astype(BF)
    grad_pre = (grad_act * (logistic * (1.0 + preact * (1.0 - logistic)))).astype(BF)
    over_samples = (((0,), (0,)), ((), ()))
    for g in range(0, shards, step):
        rows = slice(g * in_rows, (g + step) * in_rows)
        partial = lax.dot_general(grad_pre, inner(g), (((1,), (1,)), ((), ())), preferred_element_type=F32).astype(BF)
        for k, ref in enumerate(partial_refs):
            ref[:, rows] = partial[k * samples : (k + 1) * samples]
        part = lax.dot_general(joined[:, rows], grad_pre, over_samples, preferred_element_type=F32).astype(BF)
        parts_ref[g : g + step, :in_rows, :] = part.reshape(step, in_rows, -1)
        part = lax.dot_general(
            joined[:, flat + g * out_cols : flat + (g + step) * out_cols],
            activated,
            over_samples,
            preferred_element_type=F32,
        ).astype(BF)
        parts_ref[g : g + step, in_rows:, :] = part.reshape(step, out_cols, -1)


def middle(weights, pieces, in_rows):
    shards = weights.shape[0]
    samples, wide = pieces[0].shape
    whole = pl.BlockSpec(memory_space=pltpu.VMEM)
    out = pl.pallas_call(
        functools.partial(middle_kernel, shards, in_rows),
        out_shape=[jax.ShapeDtypeStruct(weights.shape, BF)]
        + [jax.ShapeDtypeStruct((samples, shards * in_rows), BF)] * 4,
        in_specs=[whole] * 5,
        out_specs=[whole] * 5,
        scratch_shapes=[pltpu.VMEM((4 * samples, wide), BF)],
        compiler_params=pltpu.CompilerParams(vmem_limit_bytes=14 * 1024 * 1024),
        cost_estimate=pl.CostEstimate(flops=1 << 30, bytes_accessed=6 << 20, transcendentals=1 << 15),
        name="middle",
    )(weights, *pieces)
    return out[0], out[1:]


def count_slots(slots, out_ref):
    width = slots.shape[1]
    high, low = slots >> 7, slots & 127
    ids = lax.broadcasted_iota(jnp.int32, (128, width), 0)
    lows = [jnp.where(ids == low[b : b + 1], 1.0, 0.0).astype(BF) for b in range(4)]
    for block in range(DEDUP // 128):
        counts = jnp.zeros((128, width), BF)
        for b in range(4):
            counts += lows[b] * jnp.where(high[b : b + 1] == block, 1.0, 0.0).astype(BF)
        out_ref[block * 128 : (block + 1) * 128, :] = counts


def segment_kernel(slots_ref, values_ref, out_ref, total_ref, even_ref, odd_ref):
    sources, _, width = slots_ref.shape
    half = width // 2

    def add(source, counts_ref):
        tail = values_ref[source, width : width + half, :]
        left = lax.broadcasted_iota(jnp.int32, tail.shape, 1) < 64
        zero = jnp.zeros_like(tail)
        values = jnp.concatenate(
            [
                jnp.concatenate([values_ref[source, :half, :], jnp.where(left, tail, zero)], axis=1),
                jnp.concatenate([values_ref[source, half:width, :], jnp.where(left, zero, tail)], axis=1),
            ]
        )
        total_ref[...] += jnp.dot(counts_ref[...], values, preferred_element_type=F32)

    total_ref[...] = jnp.zeros_like(total_ref)
    count_slots(slots_ref[0], even_ref)

    def step(j, _):
        count_slots(slots_ref[2 * j + 1], odd_ref)
        add(2 * j, even_ref)
        count_slots(slots_ref[jnp.minimum(2 * j + 2, sources - 1)], even_ref)
        add(2 * j + 1, odd_ref)
        return _

    lax.fori_loop(0, sources // 2, step, jnp.int32(0))
    out_ref[:, :128] = total_ref[:, :128].astype(BF)
    out_ref[:, 128:] = (total_ref[:, 128:192] + total_ref[:, 192:]).astype(BF)


def segment_sums(slots, values):
    width = slots.shape[2]
    whole = pl.BlockSpec(memory_space=pltpu.VMEM)
    return pl.pallas_call(
        segment_kernel,
        in_specs=[whole] * 2,
        out_specs=whole,
        scratch_shapes=[pltpu.VMEM((DEDUP, 256), F32)] + [pltpu.VMEM((DEDUP, width), BF)] * 2,
        out_shape=jax.ShapeDtypeStruct((DEDUP, 192), BF),
        compiler_params=pltpu.CompilerParams(vmem_limit_bytes=12 * 1024 * 1024),
        cost_estimate=pl.CostEstimate(flops=2 << 30, bytes_accessed=10 << 20, transcendentals=0),
        name="segment_sums",
    )(slots, values)


def add_kernel(*refs):
    total = refs[0][...].astype(F32)
    for ref in refs[1:-1]:
        total = total + ref[...].astype(F32)
    refs[-1][...] = total.astype(refs[-1].dtype)


def add_pieces(pieces, dtype):
    return pl.pallas_call(
        add_kernel,
        out_shape=jax.ShapeDtypeStruct(pieces[0].shape, dtype),
        compiler_params=pltpu.CompilerParams(vmem_limit_bytes=4 * 1024 * 1024),
        cost_estimate=pl.CostEstimate(flops=1 << 18, bytes_accessed=1 << 20, transcendentals=0),
        name="add_pieces",
    )(*pieces)


def body(pooled, projection, w_inner, w_outer, upstream, feature_order, bag_slots, bag_lengths):
    samples, features, emb_width = pooled.shape
    rank = projection.shape[1]
    shards = lax.axis_size("fsdp")
    in_rows, units = w_inner.shape
    out_cols = w_outer.shape[1]
    flat, width = in_rows * shards, out_cols * shards
    grad_rows = in_rows + out_cols
    quarter = units // 4
    rep, tab = lax.axis_index("rep"), lax.axis_index("tab")
    far, core = tab // 2, tab % 2
    place = 2 * rep + core
    mine = place % 4

    weights = jnp.concatenate(
        [
            lax.dynamic_slice(w_inner, (0, mine * quarter), (in_rows, quarter)),
            lax.dynamic_slice(w_outer.T, (0, mine * quarter), (out_cols, quarter)),
        ]
    )
    weights = spread(weights, shards, "fsdp")

    compress = jnp.einsum("bfe,fk->bek", pooled, projection, preferred_element_type=F32).astype(BF)
    zed = jnp.einsum("bfe,bek->bfk", pooled, compress, preferred_element_type=F32).astype(BF)
    joined = jnp.concatenate([zed.reshape(samples, flat), upstream], axis=1)

    bag = bag_slots.shape[-1]
    live = jnp.where(jnp.arange(bag) < bag_lengths[..., None], bag_slots, -1)
    live = live.reshape(4, 2, samples * 16, bag).transpose(0, 1, 3, 2)
    near = []
    for k in range(4):
        piece = lax.dynamic_index_in_dim(live, rep ^ k, 0, False)
        near.append(lax.ppermute(piece, "rep", [(r, r ^ k) for r in range(4)]) if k else piece)
    pieces = [joined] + [swap(joined, k) for k in (1, 2, 3)]
    slots = lax.all_gather(live, ZT)
    pieces, near = lax.optimization_barrier((pieces, near))
    parts, partial_zed = middle(weights, pieces, in_rows)
    parts = exchange(parts, "fsdp")
    slots = lax.ppermute(
        jnp.concatenate(near), ZT, [(flat_id(target(h, r, c), h, c), flat_id(h, r, c)) for h, r, c in DEVICES]
    )
    grad_zed = add_pieces([partial_zed[0]] + [swap(partial_zed[k], k) for k in (1, 2, 3)], BF)
    grad_zed = grad_zed.reshape(samples, features, rank).transpose(0, 2, 1)
    grad_comp = jnp.einsum("bfe,bkf->bke", pooled, grad_zed, preferred_element_type=F32).astype(BF)
    owners = jnp.take(jnp.array(OWNERS, jnp.int32).reshape(-1), far * 8 + jnp.arange(8))
    order = jnp.take(feature_order.reshape(8, 16), owners, axis=0).reshape(-1)
    order = (jnp.arange(features)[:, None] == order[None, :]).astype(BF)
    proj = jnp.dot(projection.T, order, preferred_element_type=F32).astype(BF)
    routed = pooled_grads(grad_zed, compress.transpose(0, 2, 1), grad_comp, order, proj, grad_rows)
    part_proj = jnp.einsum("bfe,bke->kf", pooled, grad_comp, preferred_element_type=F32)
    slots, routed, part_proj = lax.optimization_barrier((slots, routed, part_proj))
    routed = exchange(with_chunks(routed, parts, samples * 24), ZT, QUAD)
    for bit in range(shards.bit_length() - 1):
        part_proj = part_proj + lax.ppermute(part_proj, "fsdp", [(s, s ^ (1 << bit)) for s in range(shards)])
    index = jnp.arange(8, dtype=jnp.int32)
    slots = jnp.take(slots, (far ^ (index // 2)) * 2 + index % 2, axis=0)
    part_proj, routed, slots = lax.optimization_barrier((part_proj, routed, slots))

    share = routed[:, samples * 24 :].reshape(2, -1, 128).astype(F32)
    chunks = jnp.concatenate([(share[0] + share[1]).astype(BF), high_low(part_proj, 0)])
    chunks = jnp.sum(spread(chunks, 4, ZT, FAR).astype(F32), axis=0)
    proj_rows = high_low(chunks[-32:-16] + chunks[-16:], 0)
    chunks = lax.all_gather(jnp.concatenate([chunks[:-32].astype(BF), proj_rows]), ZT, axis_index_groups=QUAD)

    sums = segment_sums(slots, routed).reshape(4, DEDUP // 4, emb_width)
    landed = []
    for k in range(4):
        pairs = [(flat_id(h, r, c), flat_id(target(h, r, c), (h + k) % 4, c)) for h, r, c in DEVICES]
        landed.append(lax.ppermute(lax.dynamic_index_in_dim(sums, (far + k) % 4, 0, False), ZT, pairs))
    chunks, landed = lax.optimization_barrier((chunks, landed))
    row_share = jnp.zeros((DEDUP // 4, emb_width), F32)
    for piece in landed:
        row_share = row_share + piece.astype(F32)

    proj_sum = jnp.sum(chunks[:, -32:].astype(F32), axis=0)
    proj_sum = (proj_sum[:16] + proj_sum[16:]).T
    grads = chunks[:, :-32].reshape(8, 8, -1, 128).transpose(0, 2, 1, 3).reshape(-1, units)[:grad_rows]

    all_samples = samples * lax.axis_size("rep") * lax.axis_size("tab") * lax.axis_size("fsdp")
    loss_scale = 1.0 / math.sqrt(all_samples)
    grad_inner = grads[:in_rows].astype(F32) * loss_scale
    grad_outer = (grads[in_rows:].astype(F32) * loss_scale).T
    grad_proj = proj_sum * loss_scale
    row_grads = row_share.reshape(1, 1, DEDUP // 4, emb_width)
    return (grad_inner, grad_outer, grad_proj, row_grads)


def solution(mesh):
    in_specs = (
        P(("rep", "tab", "fsdp"), None, None),
        P(),
        P("fsdp", None),
        P(None, "fsdp"),
        P(("rep", "tab", "fsdp"), None),
        P(),
        P("rep", None, "fsdp", "tab", None),
        P("rep", None, "fsdp", "tab"),
    )
    out_specs = (P("fsdp", None), P(None, "fsdp"), P(), P("tab", "fsdp", "rep", None))
    return jax.shard_map(body, mesh=mesh, in_specs=in_specs, out_specs=out_specs, check_vma=False)
```

```python
import functools
import math

import jax
import jax.numpy as jnp
from jax import lax
from jax.experimental import pallas as pl
from jax.experimental.pallas import tpu as pltpu
from jax.sharding import PartitionSpec as P

DEDUP = 1024
BF = jnp.bfloat16
F32 = jnp.float32
ZT = ("rep", "tab")
N_REP, N_TAB = 4, 8
TEAM = [[(2 * a + b) * 8 + 2 * h + c for b in range(2) for c in range(2)] for a in range(2) for h in range(4)]
QUAD = [[r * 8 + 2 * h + c for r in range(4) for c in range(2)] for h in range(4)]
FAR = [[r * 8 + 2 * h + c for h in range(4)] for r in range(4) for c in range(2)]


def target(quad, rep, core):
    middle = 0 if (rep == 1) == (core == 0) else 2
    return (quad + {0: 3, 3: 1}.get(rep, middle)) % 4


DEVICES = [(h, r, c) for h in range(4) for r in range(4) for c in range(2)]


def flat_id(quad, rep, core):
    return rep * 8 + 2 * quad + core


def exchange(pieces, axis, groups=None):
    return lax.all_to_all(pieces, axis, 0, 0, axis_index_groups=groups)


def spread(block, count, axis, groups=None):
    return exchange(jnp.broadcast_to(block[None], (count,) + block.shape), axis, groups)


def high_low(values, axis):
    high = values.astype(BF)
    return jnp.concatenate([high, (values - high.astype(F32)).astype(BF)], axis=axis)


def swap(block, k):
    pairs = [(r * 8 + t, (r ^ (k >> 1)) * 8 + (t ^ (k & 1))) for r in range(N_REP) for t in range(N_TAB)]
    return lax.ppermute(block, ZT, pairs)


def pooled_kernel(grads_ref, compress_ref, comp_ref, order_ref, proj_ref, out_ref, ordered_ref):
    samples = compress_ref.shape[0]
    half = samples // 2
    rank = proj_ref.shape[0]
    down = (((0,), (0,)), ((), ()))
    whole = grads_ref[...].reshape(samples * rank, 128)
    ordered = jnp.dot(whole, order_ref[...], preferred_element_type=F32).astype(BF)
    ordered_ref[...] = ordered.reshape(samples, rank, 128)

    def step(i, _):
        both = []
        for sample in (i, i + half):
            left = jnp.concatenate([ordered_ref[sample], proj_ref[...]], axis=0)
            right = jnp.concatenate([compress_ref[sample], comp_ref[sample]], axis=0)
            grads = lax.dot_general(left, right, down, preferred_element_type=F32).astype(BF)
            rows = pl.ds(pl.multiple_of(sample * 16, 16), 16)
            for p in range(8):
                out_ref[p, rows, :] = grads[16 * p : 16 * p + 16, :128]
            both.append(grads[:, 128:])
        tail = jnp.concatenate(both, axis=1)
        rows = pl.ds(pl.multiple_of(samples * 16 + i * 16, 16), 16)
        for p in range(8):
            out_ref[p, rows, :] = tail[16 * p : 16 * p + 16, :]
        return _

    lax.fori_loop(0, half, step, jnp.int32(0), unroll=4)
    first = samples * 24
    out_ref[:, first:, :] = jnp.zeros((8, out_ref.shape[1] - first, 128), BF)


def pooled_grads(grad_zed, compress, grad_comp, order, proj, grad_rows):
    samples, rank, _ = grad_zed.shape
    chunk = chunk_rows(grad_rows, samples * 24)
    whole = pl.BlockSpec(memory_space=pltpu.VMEM)
    return pl.pallas_call(
        pooled_kernel,
        out_shape=jax.ShapeDtypeStruct((8, samples * 24 + 2 * chunk, 128), BF),
        in_specs=[whole] * 5,
        out_specs=whole,
        scratch_shapes=[pltpu.VMEM((samples, rank, 128), BF)],
        compiler_params=pltpu.CompilerParams(vmem_limit_bytes=12 * 1024 * 1024),
        cost_estimate=pl.CostEstimate(flops=2 * samples * 128 * 256 * 128, bytes_accessed=6 << 20, transcendentals=0),
        name="pooled_grads",
    )(grad_zed, compress, grad_comp, order, proj)


def chunk_rows(grad_rows, first):
    return next(c for c in range(16, first, 16) if 8 * c >= grad_rows and first % (2 * c) == 0)


def chunk_kernel(parts_ref, routed_ref, out_ref):
    del routed_ref
    grad_rows = parts_ref.shape[1]
    chunk = out_ref.shape[1] // 2
    for p in range(8):
        rows = min(chunk, grad_rows - p * chunk)
        if rows <= 0:
            out_ref[p] = jnp.zeros((2 * chunk, 128), BF)
            continue
        total = jnp.sum(parts_ref[:, p * chunk : p * chunk + rows, :].astype(F32), axis=0).astype(BF)
        out_ref[p, :rows, :] = total[:, :128]
        out_ref[p, chunk : chunk + rows, :] = total[:, 128:]


def with_chunks(routed, parts, first):
    chunk = chunk_rows(parts.shape[1], first)
    return pl.pallas_call(
        chunk_kernel,
        grid=(1,),
        out_shape=jax.ShapeDtypeStruct(routed.shape, BF),
        in_specs=[pl.BlockSpec(parts.shape, lambda i: (0, 0, 0)), pl.BlockSpec(memory_space=pl.ANY)],
        out_specs=pl.BlockSpec((8, 2 * chunk, 128), lambda i: (0, first // (2 * chunk), 0)),
        input_output_aliases={1: 0},
        compiler_params=pltpu.CompilerParams(vmem_limit_bytes=10 * 1024 * 1024),
        cost_estimate=pl.CostEstimate(flops=1 << 20, bytes_accessed=2 << 20, transcendentals=0),
        name="with_chunks",
    )(parts, routed)


def middle_kernel(shards, in_rows, weights_ref, *refs):
    pieces, (parts_ref, *partial_refs), joined = refs[:4], refs[4:7], refs[7]
    samples = pieces[0].shape[0]
    flat = shards * in_rows
    out_cols = weights_ref.shape[1] - in_rows
    step = 4 if shards % 4 == 0 else 1
    for k, piece in enumerate(pieces):
        joined[k * samples : (k + 1) * samples, :] = piece[...]

    def inner(g):
        return weights_ref[g : g + step, :in_rows, :].reshape(step * in_rows, -1)

    preact = jnp.zeros((4 * samples, weights_ref.shape[2]), F32)
    grad_act = jnp.zeros_like(preact)
    for g in range(0, shards, step):
        preact += jnp.dot(joined[:, g * in_rows : (g + step) * in_rows], inner(g), preferred_element_type=F32)
        grad_act += jnp.dot(
            joined[:, flat + g * out_cols : flat + (g + step) * out_cols],
            weights_ref[g : g + step, in_rows:, :].reshape(step * out_cols, -1),
            preferred_element_type=F32,
        )
    logistic = jax.nn.sigmoid(preact)
    activated = (preact * logistic).astype(BF)
    grad_pre = (grad_act * (logistic * (1.0 + preact * (1.0 - logistic)))).astype(BF)
    over_samples = (((0,), (0,)), ((), ()))
    for g in range(0, shards, step):
        rows = slice(g * in_rows, (g + step) * in_rows)
        partial = lax.dot_general(grad_pre, inner(g), (((1,), (1,)), ((), ())), preferred_element_type=F32).astype(BF)
        for k in range(4):
            partial_refs[k % 2][k // 2 * samples : (k // 2 + 1) * samples, rows] = partial[k * samples : (k + 1) * samples]
        part = lax.dot_general(joined[:, rows], grad_pre, over_samples, preferred_element_type=F32).astype(BF)
        parts_ref[g : g + step, :in_rows, :] = part.reshape(step, in_rows, -1)
        part = lax.dot_general(
            joined[:, flat + g * out_cols : flat + (g + step) * out_cols],
            activated,
            over_samples,
            preferred_element_type=F32,
        ).astype(BF)
        parts_ref[g : g + step, in_rows:, :] = part.reshape(step, out_cols, -1)


def middle(weights, pieces, in_rows):
    shards = weights.shape[0]
    samples, wide = pieces[0].shape
    whole = pl.BlockSpec(memory_space=pltpu.VMEM)
    out = pl.pallas_call(
        functools.partial(middle_kernel, shards, in_rows),
        out_shape=[jax.ShapeDtypeStruct(weights.shape, BF)]
        + [jax.ShapeDtypeStruct((2 * samples, shards * in_rows), BF)] * 2,
        in_specs=[whole] * 5,
        out_specs=[whole] * 3,
        scratch_shapes=[pltpu.VMEM((4 * samples, wide), BF)],
        compiler_params=pltpu.CompilerParams(vmem_limit_bytes=14 * 1024 * 1024),
        cost_estimate=pl.CostEstimate(flops=1 << 30, bytes_accessed=6 << 20, transcendentals=1 << 15),
        name="middle",
    )(weights, *pieces)
    return out[0], out[1:]


def count_slots(slots, out_ref):
    width = slots.shape[1]
    high, low = slots >> 7, slots & 127
    ids = lax.broadcasted_iota(jnp.int32, (128, width), 0)
    lows = [jnp.where(ids == low[b : b + 1], 1.0, 0.0).astype(BF) for b in range(4)]
    for block in range(DEDUP // 128):
        counts = jnp.zeros((128, width), BF)
        for b in range(4):
            counts += lows[b] * jnp.where(high[b : b + 1] == block, 1.0, 0.0).astype(BF)
        out_ref[block * 128 : (block + 1) * 128, :] = counts


def segment_kernel(slots_ref, values_ref, out_ref, total_ref, even_ref, odd_ref):
    sources, _, width = slots_ref.shape
    half = width // 2

    def add(source, counts_ref):
        tail = values_ref[source, width : width + half, :]
        left = lax.broadcasted_iota(jnp.int32, tail.shape, 1) < 64
        zero = jnp.zeros_like(tail)
        values = jnp.concatenate(
            [
                jnp.concatenate([values_ref[source, :half, :], jnp.where(left, tail, zero)], axis=1),
                jnp.concatenate([values_ref[source, half:width, :], jnp.where(left, zero, tail)], axis=1),
            ]
        )
        total_ref[...] += jnp.dot(counts_ref[...], values, preferred_element_type=F32)

    total_ref[...] = jnp.zeros_like(total_ref)
    count_slots(slots_ref[0], even_ref)

    def step(j, _):
        count_slots(slots_ref[2 * j + 1], odd_ref)
        add(2 * j, even_ref)
        count_slots(slots_ref[jnp.minimum(2 * j + 2, sources - 1)], even_ref)
        add(2 * j + 1, odd_ref)
        return _

    lax.fori_loop(0, sources // 2, step, jnp.int32(0))
    out_ref[:, :128] = total_ref[:, :128].astype(BF)
    out_ref[:, 128:] = (total_ref[:, 128:192] + total_ref[:, 192:]).astype(BF)


def segment_sums(slots, values):
    width = slots.shape[2]
    whole = pl.BlockSpec(memory_space=pltpu.VMEM)
    return pl.pallas_call(
        segment_kernel,
        in_specs=[whole] * 2,
        out_specs=whole,
        scratch_shapes=[pltpu.VMEM((DEDUP, 256), F32)] + [pltpu.VMEM((DEDUP, width), BF)] * 2,
        out_shape=jax.ShapeDtypeStruct((DEDUP, 192), BF),
        compiler_params=pltpu.CompilerParams(vmem_limit_bytes=12 * 1024 * 1024),
        cost_estimate=pl.CostEstimate(flops=2 << 30, bytes_accessed=10 << 20, transcendentals=0),
        name="segment_sums",
    )(slots, values)


def add_kernel(mine_ref, other_ref, stay_ref, away_ref):
    rows = stay_ref.shape[0]
    total = mine_ref[...].astype(F32) + other_ref[...].astype(F32)
    stay_ref[...] = total[:rows]
    away_ref[...] = total[rows:].astype(BF)


def add_halves(mine, other):
    half = (mine.shape[0] // 2, mine.shape[1])
    whole = pl.BlockSpec(memory_space=pltpu.VMEM)
    return pl.pallas_call(
        add_kernel,
        out_shape=[jax.ShapeDtypeStruct(half, F32), jax.ShapeDtypeStruct(half, BF)],
        in_specs=[whole] * 2,
        out_specs=[whole] * 2,
        compiler_params=pltpu.CompilerParams(vmem_limit_bytes=4 * 1024 * 1024),
        cost_estimate=pl.CostEstimate(flops=1 << 18, bytes_accessed=1 << 20, transcendentals=0),
        name="add_halves",
    )(mine, other)


def row_ids_kernel(slots_ref, out_ref):
    rows, samples = slots_ref.shape
    groups, lanes = out_ref.shape
    slots = slots_ref[...]
    lane = lax.broadcasted_iota(jnp.int32, (samples, lanes), 1)
    widen = (lane // 16 == lax.broadcasted_iota(jnp.int32, (samples, lanes), 0)).astype(F32).astype(BF)
    row = lax.broadcasted_iota(jnp.int32, (rows, lanes), 0)
    own = ((row // 4) % 16 == lax.broadcasted_iota(jnp.int32, (rows, lanes), 1) % 16).astype(F32)
    row = lax.broadcasted_iota(jnp.int32, (groups, rows), 1)
    group = lax.broadcasted_iota(jnp.int32, (groups, rows), 0)
    gather = (row // 64 * 4 + row % 4 == group).astype(F32).astype(BF)

    def moved(values):
        values = jnp.dot(values.astype(F32).astype(BF), widen, preferred_element_type=F32) * own
        return jnp.dot(gather, values.astype(BF), preferred_element_type=F32)

    out_ref[...] = (moved(slots >> 5) * 32.0 + moved(slots & 31)).astype(jnp.int32)


def row_ids(slots):
    rows, samples = slots.shape
    whole = pl.BlockSpec(memory_space=pltpu.VMEM)
    return pl.pallas_call(
        row_ids_kernel,
        out_shape=jax.ShapeDtypeStruct((rows // 16, samples * 16), jnp.int32),
        in_specs=[whole],
        out_specs=whole,
        compiler_params=pltpu.CompilerParams(vmem_limit_bytes=12 * 1024 * 1024),
        cost_estimate=pl.CostEstimate(flops=1 << 25, bytes_accessed=1 << 20, transcendentals=0),
        name="row_ids",
    )(slots)


def finish_kernel(loss_scale, chunks_ref, inner_ref, outer_ref, proj_ref):
    in_rows, grad_rows = inner_ref.shape[0], inner_ref.shape[0] + outer_ref.shape[0]
    chunk = (chunks_ref.shape[1] - 32) // 8
    proj = jnp.zeros(proj_ref.shape, F32)
    for p in range(8):
        first, last = p * chunk, min((p + 1) * chunk, grad_rows)
        for ref, low, high in ((inner_ref, 0, in_rows), (outer_ref, in_rows, grad_rows)):
            a, b = max(first, low), min(last, high)
            if a < b:
                for m in range(8):
                    rows = chunks_ref[p, m * chunk + a - first : m * chunk + b - first, :]
                    ref[a - low : b - low, m * 128 : (m + 1) * 128] = rows.astype(F32) * loss_scale
        proj = proj + (chunks_ref[p, 8 * chunk : 8 * chunk + 16, :].astype(F32) + chunks_ref[p, 8 * chunk + 16 :, :].astype(F32))
    proj_ref[...] = proj * loss_scale


def finish(chunks, in_rows, out_cols, units, loss_scale):
    whole = pl.BlockSpec(memory_space=pltpu.VMEM)
    shapes = [(in_rows, units), (out_cols, units), (16, 128)]
    return pl.pallas_call(
        functools.partial(finish_kernel, loss_scale),
        out_shape=[jax.ShapeDtypeStruct(shape, F32) for shape in shapes],
        in_specs=[whole],
        out_specs=[whole] * 3,
        compiler_params=pltpu.CompilerParams(vmem_limit_bytes=24 * 1024 * 1024),
        cost_estimate=pl.CostEstimate(flops=1 << 20, bytes_accessed=2 << 20, transcendentals=0),
        name="finish",
    )(chunks)


def body(pooled, projection, w_inner, w_outer, upstream, feature_order, bag_slots, bag_lengths):
    samples, features, emb_width = pooled.shape
    rank = projection.shape[1]
    shards = lax.axis_size("fsdp")
    in_rows, units = w_inner.shape
    out_cols = w_outer.shape[1]
    flat, width = in_rows * shards, out_cols * shards
    grad_rows = in_rows + out_cols
    quarter = units // 4
    rep, tab = lax.axis_index("rep"), lax.axis_index("tab")
    far, core = tab // 2, tab % 2
    mine = (2 * rep + core) % 4

    weights = jnp.concatenate(
        [
            lax.dynamic_slice(w_inner, (0, mine * quarter), (in_rows, quarter)),
            lax.dynamic_slice(w_outer.T, (0, mine * quarter), (out_cols, quarter)),
        ]
    )
    weights = spread(weights, shards, "fsdp")

    compress = jnp.einsum("bfe,fk->bek", pooled, projection, preferred_element_type=F32).astype(BF)
    zed = jnp.einsum("bfe,bek->bfk", pooled, compress, preferred_element_type=F32).astype(BF)
    joined = jnp.concatenate([zed.reshape(samples, flat), upstream], axis=1)

    bag = bag_slots.shape[-1]
    live = jnp.where(jnp.arange(bag) < bag_lengths[..., None], bag_slots, -1)
    live = row_ids(live.transpose(0, 1, 3, 4, 2).reshape(-1, samples)).reshape(4, 2, bag, -1)
    near = []
    for k in range(4):
        piece = lax.dynamic_index_in_dim(live, rep ^ k, 0, False)
        near.append(lax.ppermute(piece, "rep", [(r, r ^ k) for r in range(4)]) if k else piece)
    pieces = [joined] + [swap(joined, k) for k in (1, 2, 3)]
    slots = lax.all_gather(live, ZT)
    base = (jnp.arange(features)[:, None] == feature_order[None, :]).astype(BF)
    place = jnp.arange(features)[None, :] // 16
    middle_of = jnp.where((place // 2 == 1) == (place % 2 == 0), 0, 2)
    quad = (far + jnp.where(place < 2, 3, jnp.where(place >= 6, 1, middle_of))) % 4
    slot = jnp.arange(features)[:, None]
    moved = (slot == (2 * quad + place % 2) * 16 + jnp.arange(features)[None, :] % 16).astype(BF)
    order = jnp.dot(base, moved, preferred_element_type=F32).astype(BF)
    proj = jnp.dot(projection.T, order, preferred_element_type=F32).astype(BF)
    pieces, near, order, proj = lax.optimization_barrier((pieces, near, order, proj))
    parts, partial_zed = middle(weights, pieces, in_rows)
    parts = exchange(parts, "fsdp")
    slots = lax.ppermute(
        jnp.concatenate(near),
        ZT, [(flat_id(target(h, r, c), h, c), flat_id(h, r, c)) for h, r, c in DEVICES],
    )
    stay, away = add_halves(partial_zed[0], swap(partial_zed[1], 1))
    grad_zed = stay + swap(away, 2).astype(F32)
    grad_zed = grad_zed.astype(BF)
    grad_zed = grad_zed.reshape(samples, features, rank).transpose(0, 2, 1)
    grad_comp = jnp.einsum("bfe,bkf->bke", pooled, grad_zed, preferred_element_type=F32).astype(BF)
    routed = pooled_grads(grad_zed, compress.transpose(0, 2, 1), grad_comp, order, proj, grad_rows)
    part_proj = jnp.einsum("bfe,bke->kf", pooled, grad_comp, preferred_element_type=F32)
    slots, routed, part_proj = lax.optimization_barrier((slots, routed, part_proj))
    routed = exchange(with_chunks(routed, parts, samples * 24), ZT, QUAD)
    for bit in range(shards.bit_length() - 1):
        part_proj = part_proj + lax.ppermute(part_proj, "fsdp", [(s, s ^ (1 << bit)) for s in range(shards)])
    index = jnp.arange(8, dtype=jnp.int32)
    slots = jnp.take(slots, (far ^ (index // 2)) * 2 + index % 2, axis=0)
    part_proj, routed, slots = lax.optimization_barrier((part_proj, routed, slots))

    share = routed[:, samples * 24 :].reshape(2, -1, 128).astype(F32)
    chunks = jnp.concatenate([(share[0] + share[1]).astype(BF), high_low(part_proj, 0)])
    chunks = jnp.sum(spread(chunks, 4, ZT, FAR).astype(F32), axis=0)
    proj_rows = high_low(chunks[-32:-16] + chunks[-16:], 0)
    chunks = lax.all_gather(jnp.concatenate([chunks[:-32].astype(BF), proj_rows]), ZT, axis_index_groups=QUAD)

    sums = segment_sums(slots, routed).reshape(4, DEDUP // 4, emb_width)
    landed = []
    for k in range(4):
        pairs = [(flat_id(h, r, c), flat_id(target(h, r, c), (h + k) % 4, c)) for h, r, c in DEVICES]
        landed.append(lax.ppermute(lax.dynamic_index_in_dim(sums, (far + k) % 4, 0, False), ZT, pairs))
    chunks, landed = lax.optimization_barrier((chunks, landed))
    row_share = jnp.zeros((DEDUP // 4, emb_width), F32)
    for piece in landed:
        row_share = row_share + piece.astype(F32)

    all_samples = samples * lax.axis_size("rep") * lax.axis_size("tab") * lax.axis_size("fsdp")
    loss_scale = 1.0 / math.sqrt(all_samples)
    grad_inner, grad_outer, grad_proj = finish(chunks, in_rows, out_cols, units, loss_scale)
    row_grads = row_share.reshape(1, 1, DEDUP // 4, emb_width)
    return (grad_inner, grad_outer.T, grad_proj.T, row_grads)


def solution(mesh):
    in_specs = (
        P(("rep", "tab", "fsdp"), None, None),
        P(),
        P("fsdp", None),
        P(None, "fsdp"),
        P(("rep", "tab", "fsdp"), None),
        P(),
        P("rep", None, "fsdp", "tab", None),
        P("rep", None, "fsdp", "tab"),
    )
    out_specs = (P("fsdp", None), P(None, "fsdp"), P(), P("tab", "fsdp", "rep", None))
    return jax.shard_map(body, mesh=mesh, in_specs=in_specs, out_specs=out_specs, check_vma=False)
```

```python
import functools
import math

import jax
import jax.numpy as jnp
from jax import lax
from jax.experimental import pallas as pl
from jax.experimental.pallas import tpu as pltpu
from jax.sharding import PartitionSpec as P

DEDUP = 1024
BF = jnp.bfloat16
F32 = jnp.float32
ZT = ("rep", "tab")
N_REP, N_TAB = 4, 8
TEAM = [[(2 * a + b) * 8 + 2 * h + c for b in range(2) for c in range(2)] for a in range(2) for h in range(4)]
QUAD = [[r * 8 + 2 * h + c for r in range(4) for c in range(2)] for h in range(4)]
FAR = [[r * 8 + 2 * h + c for h in range(4)] for r in range(4) for c in range(2)]


def target(quad, rep, core):
    middle = 0 if (rep == 1) == (core == 0) else 2
    return (quad + {0: 3, 3: 1}.get(rep, middle)) % 4


DEVICES = [(h, r, c) for h in range(4) for r in range(4) for c in range(2)]


def flat_id(quad, rep, core):
    return rep * 8 + 2 * quad + core


def exchange(pieces, axis, groups=None):
    return lax.all_to_all(pieces, axis, 0, 0, axis_index_groups=groups)


def spread(block, count, axis, groups=None):
    return exchange(jnp.broadcast_to(block[None], (count,) + block.shape), axis, groups)


def high_low(values, axis):
    high = values.astype(BF)
    return jnp.concatenate([high, (values - high.astype(F32)).astype(BF)], axis=axis)


def swap(block, k):
    pairs = [(r * 8 + t, (r ^ (k >> 1)) * 8 + (t ^ (k & 1))) for r in range(N_REP) for t in range(N_TAB)]
    return lax.ppermute(block, ZT, pairs)


def pooled_kernel(grads_ref, compress_ref, comp_ref, order_ref, proj_ref, out_ref, ordered_ref):
    samples = compress_ref.shape[0]
    half = samples // 2
    rank = proj_ref.shape[0]
    down = (((0,), (0,)), ((), ()))
    whole = grads_ref[...].reshape(samples * rank, 128)
    ordered = jnp.dot(whole, order_ref[...], preferred_element_type=F32).astype(BF)
    ordered_ref[...] = ordered.reshape(samples, rank, 128)

    def step(i, _):
        both = []
        for sample in (i, i + half):
            left = jnp.concatenate([ordered_ref[sample], proj_ref[...]], axis=0)
            right = jnp.concatenate([compress_ref[sample], comp_ref[sample]], axis=0)
            grads = lax.dot_general(left, right, down, preferred_element_type=F32).astype(BF)
            rows = pl.ds(pl.multiple_of(sample * 16, 16), 16)
            for p in range(8):
                out_ref[p, rows, :] = grads[16 * p : 16 * p + 16, :128]
            both.append(grads[:, 128:])
        tail = jnp.concatenate(both, axis=1)
        rows = pl.ds(pl.multiple_of(samples * 16 + i * 16, 16), 16)
        for p in range(8):
            out_ref[p, rows, :] = tail[16 * p : 16 * p + 16, :]
        return _

    lax.fori_loop(0, half, step, jnp.int32(0), unroll=4)
    first = samples * 24
    out_ref[:, first:, :] = jnp.zeros((8, out_ref.shape[1] - first, 128), BF)


def pooled_grads(grad_zed, compress, grad_comp, order, proj, grad_rows):
    samples, rank, _ = grad_zed.shape
    chunk = chunk_rows(grad_rows, samples * 24)
    whole = pl.BlockSpec(memory_space=pltpu.VMEM)
    return pl.pallas_call(
        pooled_kernel,
        out_shape=jax.ShapeDtypeStruct((8, samples * 24 + 2 * chunk, 128), BF),
        in_specs=[whole] * 5,
        out_specs=whole,
        scratch_shapes=[pltpu.VMEM((samples, rank, 128), BF)],
        compiler_params=pltpu.CompilerParams(vmem_limit_bytes=12 * 1024 * 1024),
        cost_estimate=pl.CostEstimate(flops=2 * samples * 128 * 256 * 128, bytes_accessed=6 << 20, transcendentals=0),
        name="pooled_grads",
    )(grad_zed, compress, grad_comp, order, proj)


def chunk_rows(grad_rows, first):
    return next(c for c in range(16, first, 16) if 8 * c >= grad_rows and first % (2 * c) == 0)


def chunk_kernel(parts_ref, routed_ref, out_ref):
    del routed_ref
    grad_rows = parts_ref.shape[1]
    chunk = out_ref.shape[1] // 2
    for p in range(8):
        rows = min(chunk, grad_rows - p * chunk)
        if rows <= 0:
            out_ref[p] = jnp.zeros((2 * chunk, 128), BF)
            continue
        total = jnp.sum(parts_ref[:, p * chunk : p * chunk + rows, :].astype(F32), axis=0).astype(BF)
        out_ref[p, :rows, :] = total[:, :128]
        out_ref[p, chunk : chunk + rows, :] = total[:, 128:]


def with_chunks(routed, parts, first):
    chunk = chunk_rows(parts.shape[1], first)
    return pl.pallas_call(
        chunk_kernel,
        grid=(1,),
        out_shape=jax.ShapeDtypeStruct(routed.shape, BF),
        in_specs=[pl.BlockSpec(parts.shape, lambda i: (0, 0, 0)), pl.BlockSpec(memory_space=pl.ANY)],
        out_specs=pl.BlockSpec((8, 2 * chunk, 128), lambda i: (0, first // (2 * chunk), 0)),
        input_output_aliases={1: 0},
        compiler_params=pltpu.CompilerParams(vmem_limit_bytes=10 * 1024 * 1024),
        cost_estimate=pl.CostEstimate(flops=1 << 20, bytes_accessed=2 << 20, transcendentals=0),
        name="with_chunks",
    )(parts, routed)


def middle_kernel(shards, in_rows, weights_ref, *refs):
    pieces, (parts_ref, *partial_refs), joined = refs[:4], refs[4:7], refs[7]
    samples = pieces[0].shape[0]
    flat = shards * in_rows
    out_cols = weights_ref.shape[1] - in_rows
    step = 4 if shards % 4 == 0 else 1
    for k, piece in enumerate(pieces):
        joined[k * samples : (k + 1) * samples, :] = piece[...]

    def inner(g):
        return weights_ref[g : g + step, :in_rows, :].reshape(step * in_rows, -1)

    preact = jnp.zeros((4 * samples, weights_ref.shape[2]), F32)
    grad_act = jnp.zeros_like(preact)
    for g in range(0, shards, step):
        preact += jnp.dot(joined[:, g * in_rows : (g + step) * in_rows], inner(g), preferred_element_type=F32)
        grad_act += jnp.dot(
            joined[:, flat + g * out_cols : flat + (g + step) * out_cols],
            weights_ref[g : g + step, in_rows:, :].reshape(step * out_cols, -1),
            preferred_element_type=F32,
        )
    logistic = jax.nn.sigmoid(preact)
    activated = (preact * logistic).astype(BF)
    grad_pre = (grad_act * (logistic * (1.0 + preact * (1.0 - logistic)))).astype(BF)
    over_samples = (((0,), (0,)), ((), ()))
    for g in range(0, shards, step):
        rows = slice(g * in_rows, (g + step) * in_rows)
        partial = lax.dot_general(grad_pre, inner(g), (((1,), (1,)), ((), ())), preferred_element_type=F32).astype(BF)
        for k in range(4):
            partial_refs[k % 2][k // 2 * samples : (k // 2 + 1) * samples, rows] = partial[k * samples : (k + 1) * samples]
        part = lax.dot_general(joined[:, rows], grad_pre, over_samples, preferred_element_type=F32).astype(BF)
        parts_ref[g : g + step, :in_rows, :] = part.reshape(step, in_rows, -1)
        part = lax.dot_general(
            joined[:, flat + g * out_cols : flat + (g + step) * out_cols],
            activated,
            over_samples,
            preferred_element_type=F32,
        ).astype(BF)
        parts_ref[g : g + step, in_rows:, :] = part.reshape(step, out_cols, -1)


def middle(weights, pieces, in_rows):
    shards = weights.shape[0]
    samples, wide = pieces[0].shape
    whole = pl.BlockSpec(memory_space=pltpu.VMEM)
    out = pl.pallas_call(
        functools.partial(middle_kernel, shards, in_rows),
        out_shape=[jax.ShapeDtypeStruct(weights.shape, BF)]
        + [jax.ShapeDtypeStruct((2 * samples, shards * in_rows), BF)] * 2,
        in_specs=[whole] * 5,
        out_specs=[whole] * 3,
        scratch_shapes=[pltpu.VMEM((4 * samples, wide), BF)],
        compiler_params=pltpu.CompilerParams(vmem_limit_bytes=14 * 1024 * 1024),
        cost_estimate=pl.CostEstimate(flops=1 << 30, bytes_accessed=6 << 20, transcendentals=1 << 15),
        name="middle",
    )(weights, *pieces)
    return out[0], out[1:]


def count_slots(slots, out_ref):
    width = slots.shape[1]
    high, low = slots >> 7, slots & 127
    ids = lax.broadcasted_iota(jnp.int32, (128, width), 0)
    lows = [jnp.where(ids == low[b : b + 1], 1.0, 0.0).astype(BF) for b in range(4)]
    for block in range(DEDUP // 128):
        counts = jnp.zeros((128, width), BF)
        for b in range(4):
            counts += lows[b] * jnp.where(high[b : b + 1] == block, 1.0, 0.0).astype(BF)
        out_ref[block * 128 : (block + 1) * 128, :] = counts


def segment_kernel(slots_ref, values_ref, out_ref, total_ref, even_ref, odd_ref):
    sources, _, width = slots_ref.shape
    half = width // 2

    def add(source, counts_ref):
        tail = values_ref[source, width : width + half, :]
        left = lax.broadcasted_iota(jnp.int32, tail.shape, 1) < 64
        zero = jnp.zeros_like(tail)
        values = jnp.concatenate(
            [
                jnp.concatenate([values_ref[source, :half, :], jnp.where(left, tail, zero)], axis=1),
                jnp.concatenate([values_ref[source, half:width, :], jnp.where(left, zero, tail)], axis=1),
            ]
        )
        total_ref[...] += jnp.dot(counts_ref[...], values, preferred_element_type=F32)

    total_ref[...] = jnp.zeros_like(total_ref)
    count_slots(slots_ref[0], even_ref)

    def step(j, _):
        count_slots(slots_ref[2 * j + 1], odd_ref)
        add(2 * j, even_ref)
        count_slots(slots_ref[jnp.minimum(2 * j + 2, sources - 1)], even_ref)
        add(2 * j + 1, odd_ref)
        return _

    lax.fori_loop(0, sources // 2, step, jnp.int32(0))
    out_ref[:, :128] = total_ref[:, :128].astype(BF)
    out_ref[:, 128:] = (total_ref[:, 128:192] + total_ref[:, 192:]).astype(BF)


def segment_sums(slots, values):
    width = slots.shape[2]
    whole = pl.BlockSpec(memory_space=pltpu.VMEM)
    return pl.pallas_call(
        segment_kernel,
        in_specs=[whole] * 2,
        out_specs=whole,
        scratch_shapes=[pltpu.VMEM((DEDUP, 256), F32)] + [pltpu.VMEM((DEDUP, width), BF)] * 2,
        out_shape=jax.ShapeDtypeStruct((DEDUP, 192), BF),
        compiler_params=pltpu.CompilerParams(vmem_limit_bytes=12 * 1024 * 1024),
        cost_estimate=pl.CostEstimate(flops=2 << 30, bytes_accessed=10 << 20, transcendentals=0),
        name="segment_sums",
    )(slots, values)


def add_kernel(mine_ref, other_ref, stay_ref, away_ref):
    rows = stay_ref.shape[0]
    total = mine_ref[...].astype(F32) + other_ref[...].astype(F32)
    stay_ref[...] = total[:rows]
    away_ref[...] = total[rows:].astype(BF)


def add_halves(mine, other):
    half = (mine.shape[0] // 2, mine.shape[1])
    whole = pl.BlockSpec(memory_space=pltpu.VMEM)
    return pl.pallas_call(
        add_kernel,
        out_shape=[jax.ShapeDtypeStruct(half, F32), jax.ShapeDtypeStruct(half, BF)],
        in_specs=[whole] * 2,
        out_specs=[whole] * 2,
        compiler_params=pltpu.CompilerParams(vmem_limit_bytes=4 * 1024 * 1024),
        cost_estimate=pl.CostEstimate(flops=1 << 18, bytes_accessed=1 << 20, transcendentals=0),
        name="add_halves",
    )(mine, other)


def row_ids_kernel(slots_ref, out_ref):
    rows, samples = slots_ref.shape
    groups, lanes = out_ref.shape
    slots = slots_ref[...]
    lane = lax.broadcasted_iota(jnp.int32, (samples, lanes), 1)
    widen = (lane // 16 == lax.broadcasted_iota(jnp.int32, (samples, lanes), 0)).astype(F32).astype(BF)
    row = lax.broadcasted_iota(jnp.int32, (rows, lanes), 0)
    own = ((row // 4) % 16 == lax.broadcasted_iota(jnp.int32, (rows, lanes), 1) % 16).astype(F32)
    row = lax.broadcasted_iota(jnp.int32, (groups, rows), 1)
    group = lax.broadcasted_iota(jnp.int32, (groups, rows), 0)
    gather = (row // 64 * 4 + row % 4 == group).astype(F32).astype(BF)

    def moved(values):
        values = jnp.dot(values.astype(F32).astype(BF), widen, preferred_element_type=F32) * own
        return jnp.dot(gather, values.astype(BF), preferred_element_type=F32)

    out_ref[...] = (moved(slots >> 5) * 32.0 + moved(slots & 31)).astype(jnp.int32)


def row_ids(slots):
    rows, samples = slots.shape
    whole = pl.BlockSpec(memory_space=pltpu.VMEM)
    return pl.pallas_call(
        row_ids_kernel,
        out_shape=jax.ShapeDtypeStruct((rows // 16, samples * 16), jnp.int32),
        in_specs=[whole],
        out_specs=whole,
        compiler_params=pltpu.CompilerParams(vmem_limit_bytes=12 * 1024 * 1024),
        cost_estimate=pl.CostEstimate(flops=1 << 25, bytes_accessed=1 << 20, transcendentals=0),
        name="row_ids",
    )(slots)


def finish_kernel(loss_scale, chunks_ref, inner_ref, outer_ref, proj_ref):
    in_rows, grad_rows = inner_ref.shape[0], inner_ref.shape[0] + outer_ref.shape[0]
    chunk = (chunks_ref.shape[1] - 32) // 8
    proj = jnp.zeros(proj_ref.shape, F32)
    for p in range(8):
        first, last = p * chunk, min((p + 1) * chunk, grad_rows)
        for ref, low, high in ((inner_ref, 0, in_rows), (outer_ref, in_rows, grad_rows)):
            a, b = max(first, low), min(last, high)
            if a < b:
                for m in range(8):
                    rows = chunks_ref[p, m * chunk + a - first : m * chunk + b - first, :]
                    ref[a - low : b - low, m * 128 : (m + 1) * 128] = rows.astype(F32) * loss_scale
        proj = proj + (chunks_ref[p, 8 * chunk : 8 * chunk + 16, :].astype(F32) + chunks_ref[p, 8 * chunk + 16 :, :].astype(F32))
    proj_ref[...] = proj * loss_scale


def finish(chunks, in_rows, out_cols, units, loss_scale):
    whole = pl.BlockSpec(memory_space=pltpu.VMEM)
    shapes = [(in_rows, units), (out_cols, units), (16, 128)]
    return pl.pallas_call(
        functools.partial(finish_kernel, loss_scale),
        out_shape=[jax.ShapeDtypeStruct(shape, F32) for shape in shapes],
        in_specs=[whole],
        out_specs=[whole] * 3,
        compiler_params=pltpu.CompilerParams(vmem_limit_bytes=24 * 1024 * 1024),
        cost_estimate=pl.CostEstimate(flops=1 << 20, bytes_accessed=2 << 20, transcendentals=0),
        name="finish",
    )(chunks)


def body(pooled, projection, w_inner, w_outer, upstream, feature_order, bag_slots, bag_lengths):
    samples, features, emb_width = pooled.shape
    rank = projection.shape[1]
    shards = lax.axis_size("fsdp")
    in_rows, units = w_inner.shape
    out_cols = w_outer.shape[1]
    flat, width = in_rows * shards, out_cols * shards
    grad_rows = in_rows + out_cols
    quarter = units // 4
    rep, tab = lax.axis_index("rep"), lax.axis_index("tab")
    far, core = tab // 2, tab % 2
    mine = (2 * rep + core) % 4

    weights = jnp.concatenate(
        [
            lax.dynamic_slice(w_inner, (0, mine * quarter), (in_rows, quarter)),
            lax.dynamic_slice(w_outer.T, (0, mine * quarter), (out_cols, quarter)),
        ]
    )
    weights = spread(weights, shards, "fsdp")

    compress = jnp.einsum("bfe,fk->bek", pooled, projection, preferred_element_type=F32).astype(BF)
    zed = jnp.einsum("bfe,bek->bfk", pooled, compress, preferred_element_type=F32).astype(BF)
    joined = jnp.concatenate([zed.reshape(samples, flat), upstream], axis=1)

    bag = bag_slots.shape[-1]
    live = jnp.where(jnp.arange(bag) < bag_lengths[..., None], bag_slots, -1)
    live = row_ids(live.transpose(0, 1, 3, 4, 2).reshape(-1, samples)).reshape(4, 2, bag, -1)
    near = []
    for k in range(4):
        piece = lax.dynamic_index_in_dim(live, rep ^ k, 0, False)
        near.append(lax.ppermute(piece, "rep", [(r, r ^ k) for r in range(4)]) if k else piece)
    pieces = [joined] + [swap(joined, k) for k in (1, 2, 3)]
    base = (jnp.arange(features)[:, None] == feature_order[None, :]).astype(BF)
    place = jnp.arange(features)[None, :] // 16
    middle_of = jnp.where((place // 2 == 1) == (place % 2 == 0), 0, 2)
    quad = (far + jnp.where(place < 2, 3, jnp.where(place >= 6, 1, middle_of))) % 4
    slot = jnp.arange(features)[:, None]
    moved = (slot == (2 * quad + place % 2) * 16 + jnp.arange(features)[None, :] % 16).astype(BF)
    order = jnp.dot(base, moved, preferred_element_type=F32).astype(BF)
    proj = jnp.dot(projection.T, order, preferred_element_type=F32).astype(BF)
    pieces, near[:3], order, proj = lax.optimization_barrier((pieces, near[:3], order, proj))
    parts, partial_zed = middle(weights, pieces, in_rows)
    parts = exchange(parts, "fsdp")
    slots = lax.ppermute(
        jnp.concatenate(near),
        ZT, [(flat_id(target(h, r, c), h, c), flat_id(h, r, c)) for h, r, c in DEVICES],
    )
    stay, away = add_halves(partial_zed[0], swap(partial_zed[1], 1))
    grad_zed = stay + swap(away, 2).astype(F32)
    grad_zed = grad_zed.astype(BF)
    grad_zed = grad_zed.reshape(samples, features, rank).transpose(0, 2, 1)
    grad_comp = jnp.einsum("bfe,bkf->bke", pooled, grad_zed, preferred_element_type=F32).astype(BF)
    routed = pooled_grads(grad_zed, compress.transpose(0, 2, 1), grad_comp, order, proj, grad_rows)
    part_proj = jnp.einsum("bfe,bke->kf", pooled, grad_comp, preferred_element_type=F32)
    slots, routed, part_proj = lax.optimization_barrier((slots, routed, part_proj))
    routed = exchange(with_chunks(routed, parts, samples * 24), ZT, QUAD)
    for bit in range(shards.bit_length() - 1):
        part_proj = part_proj + lax.ppermute(part_proj, "fsdp", [(s, s ^ (1 << bit)) for s in range(shards)])
    index = jnp.arange(8, dtype=jnp.int32)
    slots = jnp.take(slots, (far ^ (index // 2)) * 2 + index % 2, axis=0)
    part_proj, routed, slots = lax.optimization_barrier((part_proj, routed, slots))

    share = routed[:, samples * 24 :].reshape(2, -1, 128).astype(F32)
    chunks = jnp.concatenate([(share[0] + share[1]).astype(BF), high_low(part_proj, 0)])
    chunks = jnp.sum(spread(chunks, 4, ZT, FAR).astype(F32), axis=0)
    proj_rows = high_low(chunks[-32:-16] + chunks[-16:], 0)
    chunks = lax.all_gather(jnp.concatenate([chunks[:-32].astype(BF), proj_rows]), ZT, axis_index_groups=QUAD)

    sums = segment_sums(slots, routed).reshape(4, DEDUP // 4, emb_width)
    landed = []
    for k in range(4):
        pairs = [(flat_id(h, r, c), flat_id(target(h, r, c), (h + k) % 4, c)) for h, r, c in DEVICES]
        landed.append(lax.ppermute(lax.dynamic_index_in_dim(sums, (far + k) % 4, 0, False), ZT, pairs))
    chunks, landed = lax.optimization_barrier((chunks, landed))
    row_share = jnp.zeros((DEDUP // 4, emb_width), F32)
    for piece in landed:
        row_share = row_share + piece.astype(F32)

    all_samples = samples * lax.axis_size("rep") * lax.axis_size("tab") * lax.axis_size("fsdp")
    loss_scale = 1.0 / math.sqrt(all_samples)
    grad_inner, grad_outer, grad_proj = finish(chunks, in_rows, out_cols, units, loss_scale)
    row_grads = row_share.reshape(1, 1, DEDUP // 4, emb_width)
    return (grad_inner, grad_outer.T, grad_proj.T, row_grads)


def solution(mesh):
    in_specs = (
        P(("rep", "tab", "fsdp"), None, None),
        P(),
        P("fsdp", None),
        P(None, "fsdp"),
        P(("rep", "tab", "fsdp"), None),
        P(),
        P("rep", None, "fsdp", "tab", None),
        P("rep", None, "fsdp", "tab"),
    )
    out_specs = (P("fsdp", None), P(None, "fsdp"), P(), P("tab", "fsdp", "rep", None))
    return jax.shard_map(body, mesh=mesh, in_specs=in_specs, out_specs=out_specs, check_vma=False)
```

```python
import functools
import math

import jax
import jax.numpy as jnp
from jax import lax
from jax.experimental import pallas as pl
from jax.experimental.pallas import tpu as pltpu
from jax.sharding import PartitionSpec as P

DEDUP = 1024
BF = jnp.bfloat16
F32 = jnp.float32
ZT = ("rep", "tab")
N_REP, N_TAB = 4, 8
TEAM = [[(2 * a + b) * 8 + 2 * h + c for b in range(2) for c in range(2)] for a in range(2) for h in range(4)]
QUAD = [[r * 8 + 2 * h + c for r in range(4) for c in range(2)] for h in range(4)]
FAR = [[r * 8 + 2 * h + c for h in range(4)] for r in range(4) for c in range(2)]


def target(quad, rep, core):
    middle = 0 if (rep == 1) == (core == 0) else 2
    return (quad + {0: 3, 3: 1}.get(rep, middle)) % 4


DEVICES = [(h, r, c) for h in range(4) for r in range(4) for c in range(2)]


def flat_id(quad, rep, core):
    return rep * 8 + 2 * quad + core


def exchange(pieces, axis, groups=None):
    return lax.all_to_all(pieces, axis, 0, 0, axis_index_groups=groups)


def spread(block, count, axis, groups=None):
    return exchange(jnp.broadcast_to(block[None], (count,) + block.shape), axis, groups)


def high_low(values, axis):
    high = values.astype(BF)
    return jnp.concatenate([high, (values - high.astype(F32)).astype(BF)], axis=axis)


def swap(block, k):
    pairs = [(r * 8 + t, (r ^ (k >> 1)) * 8 + (t ^ (k & 1))) for r in range(N_REP) for t in range(N_TAB)]
    return lax.ppermute(block, ZT, pairs)


def pooled_kernel(grads_ref, compress_ref, comp_ref, order_ref, proj_ref, out_ref, ordered_ref):
    samples = compress_ref.shape[0]
    half = samples // 2
    rank = proj_ref.shape[0]
    down = (((0,), (0,)), ((), ()))
    whole = grads_ref[...].reshape(samples * rank, 128)
    ordered = jnp.dot(whole, order_ref[...], preferred_element_type=F32).astype(BF)
    ordered_ref[...] = ordered.reshape(samples, rank, 128)

    def step(i, _):
        both = []
        for sample in (i, i + half):
            left = jnp.concatenate([ordered_ref[sample], proj_ref[...]], axis=0)
            right = jnp.concatenate([compress_ref[sample], comp_ref[sample]], axis=0)
            grads = lax.dot_general(left, right, down, preferred_element_type=F32).astype(BF)
            rows = pl.ds(pl.multiple_of(sample * 16, 16), 16)
            for p in range(8):
                out_ref[p, rows, :] = grads[16 * p : 16 * p + 16, :128]
            both.append(grads[:, 128:])
        tail = jnp.concatenate(both, axis=1)
        rows = pl.ds(pl.multiple_of(samples * 16 + i * 16, 16), 16)
        for p in range(8):
            out_ref[p, rows, :] = tail[16 * p : 16 * p + 16, :]
        return _

    lax.fori_loop(0, half, step, jnp.int32(0), unroll=8)


def pooled_grads(grad_zed, compress, grad_comp, order, proj, grad_rows):
    samples, rank, _ = grad_zed.shape
    chunk = chunk_rows(grad_rows, samples * 24)
    whole = pl.BlockSpec(memory_space=pltpu.VMEM)
    return pl.pallas_call(
        pooled_kernel,
        out_shape=jax.ShapeDtypeStruct((8, samples * 24 + 2 * chunk, 128), BF),
        in_specs=[whole] * 5,
        out_specs=whole,
        scratch_shapes=[pltpu.VMEM((samples, rank, 128), BF)],
        compiler_params=pltpu.CompilerParams(vmem_limit_bytes=12 * 1024 * 1024),
        cost_estimate=pl.CostEstimate(flops=2 * samples * 128 * 256 * 128, bytes_accessed=6 << 20, transcendentals=0),
        name="pooled_grads",
    )(grad_zed, compress, grad_comp, order, proj)


def chunk_rows(grad_rows, first):
    return next(c for c in range(16, first, 16) if 8 * c >= grad_rows and first % (2 * c) == 0)


def chunk_kernel(parts_ref, routed_ref, out_ref):
    del routed_ref
    grad_rows = parts_ref.shape[1]
    chunk = out_ref.shape[1] // 2
    for p in range(8):
        rows = min(chunk, grad_rows - p * chunk)
        if rows <= 0:
            out_ref[p] = jnp.zeros((2 * chunk, 128), BF)
            continue
        total = jnp.sum(parts_ref[:, p * chunk : p * chunk + rows, :].astype(F32), axis=0).astype(BF)
        out_ref[p, :rows, :] = total[:, :128]
        out_ref[p, chunk : chunk + rows, :] = total[:, 128:]


def with_chunks(routed, parts, first):
    chunk = chunk_rows(parts.shape[1], first)
    return pl.pallas_call(
        chunk_kernel,
        grid=(1,),
        out_shape=jax.ShapeDtypeStruct(routed.shape, BF),
        in_specs=[pl.BlockSpec(parts.shape, lambda i: (0, 0, 0)), pl.BlockSpec(memory_space=pl.ANY)],
        out_specs=pl.BlockSpec((8, 2 * chunk, 128), lambda i: (0, first // (2 * chunk), 0)),
        input_output_aliases={1: 0},
        compiler_params=pltpu.CompilerParams(vmem_limit_bytes=10 * 1024 * 1024),
        cost_estimate=pl.CostEstimate(flops=1 << 20, bytes_accessed=2 << 20, transcendentals=0),
        name="with_chunks",
    )(parts, routed)


def middle_kernel(shards, in_rows, weights_ref, *refs):
    pieces, (parts_ref, *partial_refs), joined = refs[:4], refs[4:7], refs[7]
    samples = pieces[0].shape[0]
    flat = shards * in_rows
    out_cols = weights_ref.shape[1] - in_rows
    step = 4 if shards % 4 == 0 else 1
    for k, piece in enumerate(pieces):
        joined[k * samples : (k + 1) * samples, :] = piece[...]

    def inner(g):
        return weights_ref[g : g + step, :in_rows, :].reshape(step * in_rows, -1)

    preact = jnp.zeros((4 * samples, weights_ref.shape[2]), F32)
    grad_act = jnp.zeros_like(preact)
    for g in range(0, shards, step):
        preact += jnp.dot(joined[:, g * in_rows : (g + step) * in_rows], inner(g), preferred_element_type=F32)
        grad_act += jnp.dot(
            joined[:, flat + g * out_cols : flat + (g + step) * out_cols],
            weights_ref[g : g + step, in_rows:, :].reshape(step * out_cols, -1),
            preferred_element_type=F32,
        )
    logistic = jax.nn.sigmoid(preact)
    activated = (preact * logistic).astype(BF)
    grad_pre = (grad_act * (logistic * (1.0 + preact * (1.0 - logistic)))).astype(BF)
    over_samples = (((0,), (0,)), ((), ()))
    for g in range(0, shards, step):
        rows = slice(g * in_rows, (g + step) * in_rows)
        partial = lax.dot_general(grad_pre, inner(g), (((1,), (1,)), ((), ())), preferred_element_type=F32).astype(BF)
        for k in range(4):
            partial_refs[k % 2][k // 2 * samples : (k // 2 + 1) * samples, rows] = partial[k * samples : (k + 1) * samples]
        part = lax.dot_general(joined[:, rows], grad_pre, over_samples, preferred_element_type=F32).astype(BF)
        parts_ref[g : g + step, :in_rows, :] = part.reshape(step, in_rows, -1)
        part = lax.dot_general(
            joined[:, flat + g * out_cols : flat + (g + step) * out_cols],
            activated,
            over_samples,
            preferred_element_type=F32,
        ).astype(BF)
        parts_ref[g : g + step, in_rows:, :] = part.reshape(step, out_cols, -1)


def middle(weights, pieces, in_rows):
    shards = weights.shape[0]
    samples, wide = pieces[0].shape
    whole = pl.BlockSpec(memory_space=pltpu.VMEM)
    out = pl.pallas_call(
        functools.partial(middle_kernel, shards, in_rows),
        out_shape=[jax.ShapeDtypeStruct(weights.shape, BF)]
        + [jax.ShapeDtypeStruct((2 * samples, shards * in_rows), BF)] * 2,
        in_specs=[whole] * 5,
        out_specs=[whole] * 3,
        scratch_shapes=[pltpu.VMEM((4 * samples, wide), BF)],
        compiler_params=pltpu.CompilerParams(vmem_limit_bytes=14 * 1024 * 1024),
        cost_estimate=pl.CostEstimate(flops=1 << 30, bytes_accessed=6 << 20, transcendentals=1 << 15),
        name="middle",
    )(weights, *pieces)
    return out[0], out[1:]


def count_slots(slots, out_ref):
    width = slots.shape[1]
    high, low = slots >> 7, slots & 127
    ids = lax.broadcasted_iota(jnp.int32, (128, width), 0)
    lows = [jnp.where(ids == low[b : b + 1], 1.0, 0.0).astype(BF) for b in range(4)]
    for block in range(DEDUP // 128):
        counts = jnp.zeros((128, width), BF)
        for b in range(4):
            counts += lows[b] * jnp.where(high[b : b + 1] == block, 1.0, 0.0).astype(BF)
        out_ref[block * 128 : (block + 1) * 128, :] = counts


def segment_kernel(slots_ref, values_ref, out_ref, total_ref, even_ref, odd_ref):
    sources, _, width = slots_ref.shape
    half = width // 2

    def add(source, counts_ref):
        tail = values_ref[source, width : width + half, :]
        left = lax.broadcasted_iota(jnp.int32, tail.shape, 1) < 64
        zero = jnp.zeros_like(tail)
        values = jnp.concatenate(
            [
                jnp.concatenate([values_ref[source, :half, :], jnp.where(left, tail, zero)], axis=1),
                jnp.concatenate([values_ref[source, half:width, :], jnp.where(left, zero, tail)], axis=1),
            ]
        )
        total_ref[...] += jnp.dot(counts_ref[...], values, preferred_element_type=F32)

    total_ref[...] = jnp.zeros_like(total_ref)
    count_slots(slots_ref[0], even_ref)

    def step(j, _):
        count_slots(slots_ref[2 * j + 1], odd_ref)
        add(2 * j, even_ref)
        count_slots(slots_ref[jnp.minimum(2 * j + 2, sources - 1)], even_ref)
        add(2 * j + 1, odd_ref)
        return _

    lax.fori_loop(0, sources // 2, step, jnp.int32(0))
    out_ref[:, :128] = total_ref[:, :128].astype(BF)
    out_ref[:, 128:] = (total_ref[:, 128:192] + total_ref[:, 192:]).astype(BF)


def segment_sums(slots, values):
    width = slots.shape[2]
    whole = pl.BlockSpec(memory_space=pltpu.VMEM)
    return pl.pallas_call(
        segment_kernel,
        in_specs=[whole] * 2,
        out_specs=whole,
        scratch_shapes=[pltpu.VMEM((DEDUP, 256), F32)] + [pltpu.VMEM((DEDUP, width), BF)] * 2,
        out_shape=jax.ShapeDtypeStruct((DEDUP, 192), BF),
        compiler_params=pltpu.CompilerParams(vmem_limit_bytes=12 * 1024 * 1024),
        cost_estimate=pl.CostEstimate(flops=2 << 30, bytes_accessed=10 << 20, transcendentals=0),
        name="segment_sums",
    )(slots, values)


def add_kernel(mine_ref, other_ref, stay_ref, away_ref):
    rows = stay_ref.shape[0]
    total = mine_ref[...].astype(F32) + other_ref[...].astype(F32)
    stay_ref[...] = total[:rows]
    away_ref[...] = total[rows:].astype(BF)


def add_halves(mine, other):
    half = (mine.shape[0] // 2, mine.shape[1])
    whole = pl.BlockSpec(memory_space=pltpu.VMEM)
    return pl.pallas_call(
        add_kernel,
        out_shape=[jax.ShapeDtypeStruct(half, F32), jax.ShapeDtypeStruct(half, BF)],
        in_specs=[whole] * 2,
        out_specs=[whole] * 2,
        compiler_params=pltpu.CompilerParams(vmem_limit_bytes=4 * 1024 * 1024),
        cost_estimate=pl.CostEstimate(flops=1 << 18, bytes_accessed=1 << 20, transcendentals=0),
        name="add_halves",
    )(mine, other)


def row_ids_kernel(slots_ref, out_ref):
    rows, samples = slots_ref.shape
    groups, lanes = out_ref.shape
    slots = slots_ref[...]
    lane = lax.broadcasted_iota(jnp.int32, (samples, lanes), 1)
    widen = (lane // 16 == lax.broadcasted_iota(jnp.int32, (samples, lanes), 0)).astype(F32).astype(BF)
    row = lax.broadcasted_iota(jnp.int32, (rows, lanes), 0)
    own = ((row // 4) % 16 == lax.broadcasted_iota(jnp.int32, (rows, lanes), 1) % 16).astype(F32)
    row = lax.broadcasted_iota(jnp.int32, (groups, rows), 1)
    group = lax.broadcasted_iota(jnp.int32, (groups, rows), 0)
    gather = (row // 64 * 4 + row % 4 == group).astype(F32).astype(BF)

    def moved(values):
        values = jnp.dot(values.astype(F32).astype(BF), widen, preferred_element_type=F32) * own
        return jnp.dot(gather, values.astype(BF), preferred_element_type=F32)

    out_ref[...] = (moved(slots >> 5) * 32.0 + moved(slots & 31)).astype(jnp.int32)


def row_ids(slots):
    rows, samples = slots.shape
    whole = pl.BlockSpec(memory_space=pltpu.VMEM)
    return pl.pallas_call(
        row_ids_kernel,
        out_shape=jax.ShapeDtypeStruct((rows // 16, samples * 16), jnp.int32),
        in_specs=[whole],
        out_specs=whole,
        compiler_params=pltpu.CompilerParams(vmem_limit_bytes=12 * 1024 * 1024),
        cost_estimate=pl.CostEstimate(flops=1 << 25, bytes_accessed=1 << 20, transcendentals=0),
        name="row_ids",
    )(slots)


def finish_kernel(loss_scale, chunks_ref, inner_ref, outer_ref, proj_ref):
    in_rows, grad_rows = inner_ref.shape[0], inner_ref.shape[0] + outer_ref.shape[0]
    chunk = (chunks_ref.shape[1] - 32) // 8
    proj = jnp.zeros(proj_ref.shape, F32)
    for p in range(8):
        first, last = p * chunk, min((p + 1) * chunk, grad_rows)
        for ref, low, high in ((inner_ref, 0, in_rows), (outer_ref, in_rows, grad_rows)):
            a, b = max(first, low), min(last, high)
            if a < b:
                for m in range(8):
                    rows = chunks_ref[p, m * chunk + a - first : m * chunk + b - first, :]
                    ref[a - low : b - low, m * 128 : (m + 1) * 128] = rows.astype(F32) * loss_scale
        proj = proj + (chunks_ref[p, 8 * chunk : 8 * chunk + 16, :].astype(F32) + chunks_ref[p, 8 * chunk + 16 :, :].astype(F32))
    proj_ref[...] = proj * loss_scale


def finish(chunks, in_rows, out_cols, units, loss_scale):
    whole = pl.BlockSpec(memory_space=pltpu.VMEM)
    shapes = [(in_rows, units), (out_cols, units), (16, 128)]
    return pl.pallas_call(
        functools.partial(finish_kernel, loss_scale),
        out_shape=[jax.ShapeDtypeStruct(shape, F32) for shape in shapes],
        in_specs=[whole],
        out_specs=[whole] * 3,
        compiler_params=pltpu.CompilerParams(vmem_limit_bytes=24 * 1024 * 1024),
        cost_estimate=pl.CostEstimate(flops=1 << 20, bytes_accessed=2 << 20, transcendentals=0),
        name="finish",
    )(chunks)


def body(pooled, projection, w_inner, w_outer, upstream, feature_order, bag_slots, bag_lengths):
    samples, features, emb_width = pooled.shape
    rank = projection.shape[1]
    shards = lax.axis_size("fsdp")
    in_rows, units = w_inner.shape
    out_cols = w_outer.shape[1]
    flat, width = in_rows * shards, out_cols * shards
    grad_rows = in_rows + out_cols
    quarter = units // 4
    rep, tab = lax.axis_index("rep"), lax.axis_index("tab")
    far, core = tab // 2, tab % 2
    mine = (2 * rep + core) % 4

    weights = jnp.concatenate(
        [
            lax.dynamic_slice(w_inner, (0, mine * quarter), (in_rows, quarter)),
            lax.dynamic_slice(w_outer.T, (0, mine * quarter), (out_cols, quarter)),
        ]
    )
    weights = spread(weights, shards, "fsdp")

    compress = jnp.einsum("bfe,fk->bek", pooled, projection, preferred_element_type=F32).astype(BF)
    zed = jnp.einsum("bfe,bek->bfk", pooled, compress, preferred_element_type=F32).astype(BF)
    joined = jnp.concatenate([zed.reshape(samples, flat), upstream], axis=1)

    bag = bag_slots.shape[-1]
    live = jnp.where(jnp.arange(bag) < bag_lengths[..., None], bag_slots, -1)
    live = row_ids(live.transpose(0, 1, 3, 4, 2).reshape(-1, samples)).reshape(4, 2, bag, -1)
    near = []
    for k in range(4):
        piece = lax.dynamic_index_in_dim(live, rep ^ k, 0, False)
        near.append(lax.ppermute(piece, "rep", [(r, r ^ k) for r in range(4)]) if k else piece)
    pieces = [joined] + [swap(joined, k) for k in (1, 2, 3)]
    base = (jnp.arange(features)[:, None] == feature_order[None, :]).astype(BF)
    place = jnp.arange(features)[None, :] // 16
    middle_of = jnp.where((place // 2 == 1) == (place % 2 == 0), 0, 2)
    quad = (far + jnp.where(place < 2, 3, jnp.where(place >= 6, 1, middle_of))) % 4
    slot = jnp.arange(features)[:, None]
    moved = (slot == (2 * quad + place % 2) * 16 + jnp.arange(features)[None, :] % 16).astype(BF)
    order = jnp.dot(base, moved, preferred_element_type=F32).astype(BF)
    proj = jnp.dot(projection.T, order, preferred_element_type=F32).astype(BF)
    pieces, near[:3], order, proj = lax.optimization_barrier((pieces, near[:3], order, proj))
    parts, partial_zed = middle(weights, pieces, in_rows)
    parts = exchange(parts, "fsdp")
    slots = lax.ppermute(
        jnp.concatenate(near),
        ZT, [(flat_id(target(h, r, c), h, c), flat_id(h, r, c)) for h, r, c in DEVICES],
    )
    stay, away = add_halves(partial_zed[0], swap(partial_zed[1], 1))
    grad_zed = stay + swap(away, 2).astype(F32)
    grad_zed = grad_zed.astype(BF)
    grad_zed = grad_zed.reshape(samples, features, rank).transpose(0, 2, 1)
    grad_comp = jnp.einsum("bfe,bkf->bke", pooled, grad_zed, preferred_element_type=F32).astype(BF)
    routed = pooled_grads(grad_zed, compress.transpose(0, 2, 1), grad_comp, order, proj, grad_rows)
    part_proj = jnp.einsum("bfe,bke->kf", pooled, grad_comp, preferred_element_type=F32)
    slots, routed, part_proj = lax.optimization_barrier((slots, routed, part_proj))
    routed = exchange(with_chunks(routed, parts, samples * 24), ZT, QUAD)
    for bit in range(shards.bit_length() - 1):
        part_proj = part_proj + lax.ppermute(part_proj, "fsdp", [(s, s ^ (1 << bit)) for s in range(shards)])
    index = jnp.arange(8, dtype=jnp.int32)
    slots = jnp.take(slots, (far ^ (index // 2)) * 2 + index % 2, axis=0)
    part_proj, routed, slots = lax.optimization_barrier((part_proj, routed, slots))

    share = routed[:, samples * 24 :].reshape(2, -1, 128).astype(F32)
    chunks = jnp.concatenate([(share[0] + share[1]).astype(BF), high_low(part_proj, 0)])
    chunks = jnp.sum(spread(chunks, 4, ZT, FAR).astype(F32), axis=0)
    proj_rows = high_low(chunks[-32:-16] + chunks[-16:], 0)
    chunks = lax.all_gather(jnp.concatenate([chunks[:-32].astype(BF), proj_rows]), ZT, axis_index_groups=QUAD)

    sums = segment_sums(slots, routed).reshape(4, DEDUP // 4, emb_width)
    landed = []
    for k in range(4):
        pairs = [(flat_id(h, r, c), flat_id(target(h, r, c), (h + k) % 4, c)) for h, r, c in DEVICES]
        landed.append(lax.ppermute(lax.dynamic_index_in_dim(sums, (far + k) % 4, 0, False), ZT, pairs))
    chunks, landed = lax.optimization_barrier((chunks, landed))
    row_share = jnp.zeros((DEDUP // 4, emb_width), F32)
    for piece in landed:
        row_share = row_share + piece.astype(F32)

    all_samples = samples * lax.axis_size("rep") * lax.axis_size("tab") * lax.axis_size("fsdp")
    loss_scale = 1.0 / math.sqrt(all_samples)
    grad_inner, grad_outer, grad_proj = finish(chunks, in_rows, out_cols, units, loss_scale)
    row_grads = row_share.reshape(1, 1, DEDUP // 4, emb_width)
    return (grad_inner, grad_outer.T, grad_proj.T, row_grads)


def solution(mesh):
    in_specs = (
        P(("rep", "tab", "fsdp"), None, None),
        P(),
        P("fsdp", None),
        P(None, "fsdp"),
        P(("rep", "tab", "fsdp"), None),
        P(),
        P("rep", None, "fsdp", "tab", None),
        P("rep", None, "fsdp", "tab"),
    )
    out_specs = (P("fsdp", None), P(None, "fsdp"), P(), P("tab", "fsdp", "rep", None))
    return jax.shard_map(body, mesh=mesh, in_specs=in_specs, out_specs=out_specs, check_vma=False)
```
